32 devices in a mesh: grp: 8 (over z, y), blk: 4 (over x, core).
Axes of the slice: x: 2, y: 2, z: 4, core: 2. Of those that a mesh axis runs over, the one named last changes fastest.
Arguments:
- states: bfloat16 [65536, 768], P(('grp', 'blk')), may hold values from -6 to 6
- query_weight: bfloat16 [768, 768], replicated, may hold values from -0.21875 to 0.21875
- attempts: bfloat16 [2048, 768], P(('grp', 'blk')), may hold values from -6 to 6
- attempt_theorem: int32 [2048], P('grp'), may hold values from 0 to 15
- positive: int32 [65536], P(('grp', 'blk')), may hold values from 0 to 255
Outputs:
- loss: float32 [65536], P(('grp', 'blk'))
- grad_attempts: float32 [2048, 768], P(('grp', 'blk'))
- grad_weight: float32 [768, 768], replicated
The draws below stay inside these ranges and needn't reach their ends.
All inputs are finite; a program needn't handle non-finite values.
Results may differ from the reference program's by a relative error of at most 0.012.
Values may be sent and summed in bfloat16 or wider, within the bound.
A program may use at most 64 MiB of HBM per device.

```python
import math
import jax
import jax.numpy as jnp
import numpy as np
from jax import lax

VECTOR_DIMENSION = 768
Q_DEV = 2048
SLICE_THEOREMS = 16
ATT_SLICE = 256
QUERIES = 65536
CANDIDATE_COUNT = 2048
N_GRP = 8
N_BLK = 4


def plant(result, stream_key, low, largest):
    dims = result.shape
    index_at = [jax.random.randint(jax.random.fold_in(stream_key, axis), (), 0, dims[axis]) for axis in range(len(dims))]
    result = result.at[tuple(index_at)].set(low)
    longest = dims.index(max(dims))
    index_at[longest] = (index_at[longest] + 1) % dims[longest]
    return result.at[tuple(index_at)].set(largest)


def steps_of(key, dims, split, least, largest):
    level = 1.0
    for position, blocks in split:
        steps = jax.random.uniform(jax.random.fold_in(jax.random.fold_in(key, 6), position), (blocks,), jnp.float32, least / len(split), largest / len(split))
        level = level * jnp.repeat(jnp.exp(steps), dims[position] // blocks).reshape((-1,) + (1,) * (len(dims) - 1 - position))
    return level


def rank_table(amount, skew):
    portions = [(1 << 20) // math.isqrt(standing ** skew) + 1 for standing in range(1, amount + 1)]
    width = 1 + sum(portions) // (1 << 30)
    return np.cumsum(np.array([max(1, weight // width) for weight in portions]))


def ranked(own_key, extent, amount, slope):
    table = rank_table(amount, slope)
    lot = jax.random.randint(jax.random.fold_in(own_key, 1), extent, 0, int(table[amount - 1]))
    grade = jnp.searchsorted(jnp.asarray(table, jnp.int32), lot, side="right")
    return jax.random.permutation(jax.random.fold_in(own_key, 2), amount)[grade].astype(jnp.int32)


def normal_values(own_key, dims, width, limit, shards=(), dtype=jnp.bfloat16):
    drawn = jax.random.normal(own_key, dims, jnp.float32) * width
    if len(shards) > 0:
        drawn = steps_of(own_key, dims, shards, -0.22, 0.18) * drawn
    return jnp.clip(drawn, min=-limit, max=limit).astype(dtype)


def setup_inputs(seed: int = 0) -> dict:
    streams_of = jax.random.split(jax.random.key(seed), 6)
    states = normal_values(streams_of[0], (QUERIES, VECTOR_DIMENSION), 1.0, 6.0, ((0, 32),))
    query_weight = normal_values(streams_of[1], (VECTOR_DIMENSION, VECTOR_DIMENSION), VECTOR_DIMENSION ** -0.5, 0.21875)
    attempts = normal_values(streams_of[2], (CANDIDATE_COUNT, VECTOR_DIMENSION), 1.0, 6.0, ((0, 32),))
    attempt_theorem = plant(ranked(streams_of[3], (CANDIDATE_COUNT,), SLICE_THEOREMS, 2), jax.random.fold_in(streams_of[3], 3), 0, SLICE_THEOREMS - 1).astype(jnp.int32)
    positive = plant(jax.random.randint(streams_of[4], (QUERIES,), 0, ATT_SLICE), jax.random.fold_in(streams_of[4], 1), 0, ATT_SLICE - 1).astype(jnp.int32)
    return {"states": states, "query_weight": query_weight, "attempts": attempts, "attempt_theorem": attempt_theorem, "positive": positive}


logit_sharpness = 0.07
epsilon = 1e-06

def normalized_rows(values):
    return values * lax.rsqrt(lax.optimization_barrier(jnp.mean(values * values, axis=-1, keepdims=True)) + epsilon)

def reference(states, query_weight, attempts, attempt_theorem, positive):
    logit_multiplier = 1.0 / (logit_sharpness * VECTOR_DIMENSION)
    state_blocks = states.reshape(N_GRP, N_BLK, Q_DEV, VECTOR_DIMENSION)
    attempt_blocks = attempts.reshape(N_GRP, ATT_SLICE, VECTOR_DIMENSION)
    theorem_blocks = attempt_theorem.reshape(N_GRP, ATT_SLICE)
    positive_blocks = positive.reshape(N_GRP, N_BLK, Q_DEV)

    def slice_step(weight_sum, slice_data):
        slice_states, slice_attempts, slice_theorem, slice_positive = slice_data
        attempt_rows_float, attempt_back = jax.vjp(normalized_rows, slice_attempts.astype(jnp.float32))
        candidate_direction = attempt_rows_float.astype(jnp.bfloat16)

        def device_step(grad_sum, device_data):
            dev_states, local_matching_target = device_data
            proj = jnp.dot(dev_states, query_weight, preferred_element_type=jnp.float32)
            query_float, query_back = jax.vjp(normalized_rows, proj)
            query_unit = query_float.astype(jnp.bfloat16)
            anchor_lemma_label = jnp.take(slice_theorem, local_matching_target)
            scores = jnp.dot(query_unit, candidate_direction.T, preferred_element_type=jnp.float32) * logit_multiplier
            mask = anchor_lemma_label[:, None] == slice_theorem[None, :]
            expo = jnp.where(mask, jnp.exp(scores), 0.0)
            total = lax.optimization_barrier(jnp.sum(expo, axis=1))
            columns = lax.broadcasted_iota(jnp.int32, scores.shape, 1)
            chosen = columns == local_matching_target[:, None]
            pos_score = lax.optimization_barrier(jnp.sum(jnp.where(chosen, scores, 0.0), axis=1))
            losses = jnp.log(total) - pos_score
            weights = (expo / total[:, None] - chosen.astype(jnp.float32)).astype(jnp.bfloat16)
            grad_qunit = jnp.dot(weights, candidate_direction, preferred_element_type=jnp.float32) * logit_multiplier
            partial_term = jnp.dot(weights.T, query_unit, preferred_element_type=jnp.float32) * logit_multiplier
            partial_term = lax.optimization_barrier(partial_term.astype(jnp.bfloat16)).astype(jnp.float32)
            grad_proj = query_back(grad_qunit)[0].astype(jnp.bfloat16)
            weight_term = jnp.dot(dev_states.T, grad_proj, preferred_element_type=jnp.float32)
            return (grad_sum + partial_term, (losses, weight_term))
        start = jnp.zeros((ATT_SLICE, VECTOR_DIMENSION), jnp.float32)
        grad_sum, (losses, weight_terms) = lax.scan(device_step, start, (slice_states, slice_positive))
        grad_attempts = attempt_back(grad_sum)[0]
        return (weight_sum + lax.optimization_barrier(jnp.sum(weight_terms, axis=0)), (losses, grad_attempts))
    weight_sum, (losses, grads) = lax.scan(slice_step, jnp.zeros((VECTOR_DIMENSION, VECTOR_DIMENSION), jnp.float32), (state_blocks, attempt_blocks, theorem_blocks, positive_blocks))
    return (losses.reshape(QUERIES), grads.reshape(CANDIDATE_COUNT, VECTOR_DIMENSION), weight_sum)
```

```python
import functools

import jax
import jax.numpy as jnp
from jax import lax
from jax.experimental import pallas as pl
from jax.experimental.pallas import tpu as pltpu
from jax.sharding import PartitionSpec as P

logit_sharpness = 0.07
epsilon = 1e-06
MESH = pl.DeviceIdType.MESH
PARTS = 3
LANES = 128
TILE = 16
NT = (((1,), (1,)), ((), ()))


def stage_plan(n_grp, n_blk, rows):
    along_x = ("blk", 2, n_blk // 2)
    along_y = ("grp", 1, 2)
    along_z = ("grp", 2, n_grp // 2)
    orders = (
        (along_x, along_y, along_z),
        (along_y, along_z, along_x),
        (along_z, along_x, along_y),
    )
    plan = []
    for order in orders:
        length, stages = rows, []
        for axis, stride, size in order:
            if size == 1:
                continue
            scatter = length % (size * TILE) == 0
            stages.append((axis, stride, size, length, scatter))
            if scatter:
                length //= size
        plan.append(stages)
    return plan


def kernel(
    n_grp, n_blk, plan, chunk,
    states, weight, attempts, theorem, positive,
    loss, grad_att, grad_w,
    weight_t, unit_t, gproj_t, w_all, inv_rms, panel, panel_t,
    ga_stage, ga_recv, acc, core_send, core_recv, res, send_sems, recv_sems, *stage_bufs,
):
    queries, dim = states.shape
    own_att = attempts.shape[0]
    n_att = own_att * n_blk
    half = dim // 2
    width = dim // PARTS
    multiplier = 1.0 / (logit_sharpness * dim)
    grp = lax.axis_index("grp")
    blk = lax.axis_index("blk")
    core = lax.rem(blk, 2)
    sibling = blk + 1 - 2 * core
    used = [0]
    started = []

    def member(axis, stride, size):
        index = grp if axis == "grp" else blk
        return lax.rem(index // stride, size)

    def partner(axis, stride, size, k):
        index = grp if axis == "grp" else blk
        here = lax.rem(index // stride, size)
        there = lax.rem(here + k, size)
        return {axis: index + (there - here) * stride}, there

    def send(src, dst, device):
        n = used[0]
        used[0] += 1
        copy = pltpu.make_async_remote_copy(
            src_ref=src, dst_ref=dst, send_sem=send_sems.at[n], recv_sem=recv_sems.at[n],
            device_id=device, device_id_type=MESH,
        )
        copy.start()
        started.append(copy)
        return copy

    greeted = [("blk", 1, n_blk), ("grp", 1, 2), ("grp", 2, n_grp // 2)]
    barrier = pltpu.get_barrier_semaphore()
    count = 0
    for axis, stride, size in greeted:
        for k in range(1, size):
            pl.semaphore_signal(
                barrier, inc=1, device_id=partner(axis, stride, size, k)[0], device_id_type=MESH
            )
            count += 1

    att = attempts[...].astype(jnp.float32)
    att_r = lax.rsqrt(jnp.mean(att * att, axis=1, keepdims=True) + epsilon)
    att_unit = att * att_r
    own_rows = pl.ds(pl.multiple_of(blk * own_att, own_att), own_att)
    panel[own_rows, :] = att_unit.astype(jnp.bfloat16)
    pl.semaphore_wait(barrier, count)
    gathers = [
        send(panel.at[own_rows], panel.at[own_rows], partner("blk", 1, n_blk, k)[0])
        for k in range(1, n_blk)
    ]

    weight_t[...] = weight[...].T

    def project(step, carry):
        cols = pl.ds(pl.multiple_of(step * chunk, chunk), chunk)
        proj = lax.dot_general(
            weight_t[...], states[cols, :], NT, preferred_element_type=jnp.float32
        )
        r = lax.rsqrt(jnp.sum(proj * proj, axis=0, keepdims=True) * (1.0 / dim) + epsilon)
        inv_rms[:, cols] = r
        unit_t[:, cols] = (proj * r).astype(jnp.bfloat16)
        return carry

    lax.fori_loop(0, queries // chunk, project, 0)

    for copy in gathers:
        copy.wait_recv()
    panel_t[...] = panel[...].T
    theorem_col = jnp.broadcast_to(theorem[...].astype(jnp.float32), (8, n_att)).T[:, 0:1]

    def contrast(step, carry):
        cols = pl.ds(pl.multiple_of(step * chunk, chunk), chunk)
        unit = unit_t[:, cols]
        scores = jnp.dot(panel[...], unit, preferred_element_type=jnp.float32) * multiplier
        chosen = lax.broadcasted_iota(jnp.int32, scores.shape, 0) == positive[:, cols]
        label = jnp.sum(jnp.where(chosen, theorem_col, 0.0), axis=0, keepdims=True)
        expo = jnp.where(theorem_col == label, jnp.exp(scores), 0.0)
        total = jnp.sum(expo, axis=0, keepdims=True)
        pos_score = jnp.sum(jnp.where(chosen, scores, 0.0), axis=0, keepdims=True)
        loss[:, cols] = jnp.log(total) - pos_score
        w = (expo * (1.0 / total) - jnp.where(chosen, 1.0, 0.0)).astype(jnp.bfloat16)
        w_all[:, cols] = w
        along = jnp.sum(w.astype(jnp.float32) * scores, axis=0, keepdims=True) * (1.0 / dim)
        r = inv_rms[:, cols]
        g = jnp.dot(panel_t[...], w, preferred_element_type=jnp.float32)
        gproj_t[:, cols] = (
            g * (r * multiplier) - unit.astype(jnp.float32) * (r * along)
        ).astype(jnp.bfloat16)
        return carry

    lax.fori_loop(0, queries // chunk, contrast, 0)

    ga_t = lax.dot_general(unit_t[...], w_all[...], NT, preferred_element_type=jnp.float32)
    ga_stage[...] = (ga_t * multiplier).T.astype(jnp.bfloat16)
    ga_copies = []
    for k in range(1, n_blk):
        device, owner = partner("blk", 1, n_blk, k)
        rows = pl.ds(pl.multiple_of(owner * own_att, own_att), own_att)
        ga_copies.append(send(ga_stage.at[rows], ga_recv.at[k - 1], device))

    def weight_tile(which, part):
        rows = pl.ds(pl.multiple_of(which * half, half), half)
        tile = jnp.dot(
            gproj_t[rows, :], states[:, part * width:(part + 1) * width],
            preferred_element_type=jnp.float32,
        )
        return tile.T

    blocks = half // LANES
    bufs = [[None] * len(stages) for stages in plan]
    n = 0
    for part, stages in enumerate(plan):
        for j in range(len(stages)):
            bufs[part][j] = (stage_bufs[n], stage_bufs[n + 1])
            n += 2
    begin = [0] * PARTS
    pending = {}

    def start_stage(part, j):
        axis, stride, size, length, scatter = plan[part][j]
        stage, recv = bufs[part][j]
        here = member(axis, stride, size)
        now = begin[part]
        rows = pl.ds(pl.multiple_of(now, TILE), length)
        stage[...] = acc[part, rows, :].astype(jnp.bfloat16)
        copies = []
        for k in range(1, size):
            device, there = partner(axis, stride, size, k)
            if scatter:
                piece = length // size
                src = stage.at[pl.ds(pl.multiple_of(there * piece, TILE), piece)]
                copies.append(send(src, recv.at[k - 1], device))
            else:
                copies.append(send(stage, recv.at[here], device))
        pending[part, j] = copies

    def finish_stage(part, j):
        axis, stride, size, length, scatter = plan[part][j]
        stage, recv = bufs[part][j]
        here = member(axis, stride, size)
        for copy in pending[part, j]:
            copy.wait_recv()
        if scatter:
            piece = length // size
            begin[part] = begin[part] + here * piece
            rows = pl.ds(pl.multiple_of(begin[part], TILE), piece)
            total = acc[part, rows, :]
            for k in range(size - 1):
                total = total + recv[k].astype(jnp.float32)
        else:
            rows = pl.ds(pl.multiple_of(begin[part], TILE), length)
            recv[here] = stage[...]
            total = recv[0].astype(jnp.float32)
            for k in range(1, size):
                total = total + recv[k].astype(jnp.float32)
        acc[part, rows, :] = total

    sequence = (2, 0, 1)
    core_copies = {}
    for part in sequence:
        tile = weight_tile(1 - core, part)
        for e in range(blocks):
            core_send[part, e * width:(e + 1) * width, :] = (
                tile[:, e * LANES:(e + 1) * LANES].astype(jnp.bfloat16)
            )
        core_copies[part] = send(core_send.at[part], core_recv.at[part], {"blk": sibling})
    for part in sequence:
        tile = weight_tile(core, part)
        core_copies[part].wait_recv()
        for e in range(blocks):
            span = slice(e * width, (e + 1) * width)
            acc[part, span, :] = (
                tile[:, e * LANES:(e + 1) * LANES] + core_recv[part, span, :].astype(jnp.float32)
            )
        start_stage(part, 0)

    for copy in ga_copies:
        copy.wait_recv()
    ga = ga_stage[own_rows, :].astype(jnp.float32)
    for k in range(n_blk - 1):
        ga = ga + ga_recv[k].astype(jnp.float32)
    att = attempts[...].astype(jnp.float32)
    att_r = lax.rsqrt(jnp.mean(att * att, axis=1, keepdims=True) + epsilon)
    att_unit = att * att_r
    grad_att[...] = att_r * (ga - att_unit * jnp.mean(ga * att_unit, axis=1, keepdims=True))

    depth = len(plan[0])
    for j in range(depth):
        for part in sequence:
            finish_stage(part, j)
            if j + 1 < depth:
                start_stage(part, j + 1)

    where = {}
    for part in sequence:
        length = plan[part][0][3]
        for axis, stride, size, rows_in, scatter in plan[part]:
            length = rows_in // size if scatter else rows_in
        rows = pl.ds(pl.multiple_of(begin[part], TILE), length)
        res[core, part, rows, :] = acc[part, rows, :].astype(jnp.bfloat16)
        where[part] = begin[part]
    for j in reversed(range(depth)):
        for part in sequence:
            axis, stride, size, length, scatter = plan[part][j]
            if not scatter:
                continue
            piece = length // size
            rows = pl.ds(pl.multiple_of(where[part], TILE), piece)
            for later in range(j + 1, depth):
                for copy in pending.pop(("back", part, later), []):
                    copy.wait_recv()
            spot = res.at[core, part, rows]
            pending["back", part, j] = [
                send(spot, spot, partner(axis, stride, size, k)[0]) for k in range(1, size)
            ]
            where[part] = where[part] - member(axis, stride, size) * piece
    last = {}
    for part in sequence:
        for key in [key for key in pending if key[0] == "back" and key[1] == part]:
            for copy in pending.pop(key):
                copy.wait_recv()
        spot = res.at[core, part]
        last[part] = send(spot, spot, {"blk": sibling})

    def place(which, part):
        for e in range(blocks):
            cols = pl.ds(pl.multiple_of(which * half + e * LANES, LANES), LANES)
            grad_w[part * width:(part + 1) * width, cols] = (
                res[which, part, e * width:(e + 1) * width, :]
            )

    for part in sequence:
        place(core, part)
    for part in sequence:
        last[part].wait_recv()
        place(1 - core, part)
    for copy in started:
        copy.wait_send()


def on_device(n_grp, n_blk, states, query_weight, attempts, attempt_theorem, positive):
    queries, dim = states.shape
    own_att = attempts.shape[0]
    n_att = own_att * n_blk
    chunk = min(512, queries)
    rows = dim * (dim // 2) // PARTS // LANES
    plan = stage_plan(n_grp, n_blk, rows)
    copies = 2 * (n_blk - 1) + 2 * PARTS
    bf16, f32 = jnp.bfloat16, jnp.float32
    stage_bufs = []
    for stages in plan:
        for axis, stride, size, length, scatter in stages:
            copies += (size - 1) * (2 if scatter else 1)
            stage_bufs.append(pltpu.VMEM((length, LANES), bf16))
            if scatter:
                stage_bufs.append(pltpu.VMEM((size - 1, length // size, LANES), bf16))
            else:
                stage_bufs.append(pltpu.VMEM((size, length, LANES), bf16))
    vmem = pl.BlockSpec(memory_space=pltpu.VMEM)
    loss, grad_att, grad_w = pl.pallas_call(
        functools.partial(kernel, n_grp, n_blk, plan, chunk),
        out_shape=(
            jax.ShapeDtypeStruct((1, queries), f32),
            jax.ShapeDtypeStruct((own_att, dim), f32),
            jax.ShapeDtypeStruct((dim, dim), bf16),
        ),
        in_specs=[vmem] * 5,
        out_specs=(vmem,) * 3,
        scratch_shapes=[
            pltpu.VMEM((dim, dim), bf16),
            pltpu.VMEM((dim, queries), bf16),
            pltpu.VMEM((dim, queries), bf16),
            pltpu.VMEM((n_att, queries), bf16),
            pltpu.VMEM((1, queries), f32),
            pltpu.VMEM((n_att, dim), bf16),
            pltpu.VMEM((dim, n_att), bf16),
            pltpu.VMEM((n_att, dim), bf16),
            pltpu.VMEM((n_blk - 1, own_att, dim), bf16),
            pltpu.VMEM((PARTS, rows, LANES), f32),
            pltpu.VMEM((PARTS, rows, LANES), bf16),
            pltpu.VMEM((PARTS, rows, LANES), bf16),
            pltpu.VMEM((2, PARTS, rows, LANES), bf16),
            pltpu.SemaphoreType.DMA((copies,)),
            pltpu.SemaphoreType.DMA((copies,)),
            *stage_bufs,
        ],
        compiler_params=pltpu.CompilerParams(
            collective_id=0, has_side_effects=True, vmem_limit_bytes=48 * 1024 * 1024
        ),
    )(states, query_weight, attempts, attempt_theorem.reshape(1, n_att), positive.reshape(1, queries))
    return loss.reshape(queries), grad_att, grad_w.astype(f32)


def solution(mesh):
    n_grp, n_blk = mesh.shape["grp"], mesh.shape["blk"]
    in_specs = (P(("grp", "blk"), None), P(), P(("grp", "blk"), None), P("grp"), P(("grp", "blk")))
    out_specs = (P(("grp", "blk")), P(("grp", "blk"), None), P())
    return jax.shard_map(
        functools.partial(on_device, n_grp, n_blk),
        mesh=mesh, in_specs=in_specs, out_specs=out_specs, check_vma=False,
    )
```

```python
import functools

import jax
import jax.numpy as jnp
from jax import lax
from jax.experimental import pallas as pl
from jax.experimental.pallas import tpu as pltpu
from jax.sharding import PartitionSpec as P

logit_sharpness = 0.07
epsilon = 1e-06
MESH = pl.DeviceIdType.MESH
PARTS = 3
LANES = 128
TILE = 16
NT = (((1,), (1,)), ((), ()))


def stage_plan(n_grp, n_blk, rows):
    along_x = ("blk", 2, n_blk // 2)
    along_y = ("grp", 1, 2)
    along_z = ("grp", 2, n_grp // 2)
    orders = (
        (along_x, along_y, along_z),
        (along_y, along_z, along_x),
        (along_z, along_x, along_y),
    )
    plan = []
    for order in orders:
        length, stages = rows, []
        for axis, stride, size in order:
            if size == 1:
                continue
            scatter = length % (size * TILE) == 0
            stages.append((axis, stride, size, length, scatter))
            if scatter:
                length //= size
        plan.append(stages)
    return plan


def kernel(
    n_grp, n_blk, plan, chunk,
    states_hbm, weight_hbm, attempts_hbm, theorem_hbm, positive_hbm,
    loss, grad_att, grad_w,
    states, weight, attempts, theorem, positive, load_sems,
    weight_t, unit_t, gproj_t, w_all, inv_rms, panel, panel_t,
    ga_stage, ga_recv, acc, core_send, core_recv, res, send_sems, recv_sems, *stage_bufs,
):
    queries, dim = states.shape
    own_att = attempts.shape[0]
    n_att = own_att * n_blk
    half = dim // 2
    width = dim // PARTS
    multiplier = 1.0 / (logit_sharpness * dim)
    grp = lax.axis_index("grp")
    blk = lax.axis_index("blk")
    core = lax.rem(blk, 2)
    sibling = blk + 1 - 2 * core
    used = [0]
    started = []

    def member(axis, stride, size):
        index = grp if axis == "grp" else blk
        return lax.rem(index // stride, size)

    def partner(axis, stride, size, k):
        index = grp if axis == "grp" else blk
        here = lax.rem(index // stride, size)
        there = lax.rem(here + k, size)
        return {axis: index + (there - here) * stride}, there

    def send(src, dst, device):
        n = used[0]
        used[0] += 1
        copy = pltpu.make_async_remote_copy(
            src_ref=src, dst_ref=dst, send_sem=send_sems.at[n], recv_sem=recv_sems.at[n],
            device_id=device, device_id_type=MESH,
        )
        copy.start()
        started.append(copy)
        return copy

    def load(src, dst, n):
        return pltpu.make_async_copy(src, dst, load_sems.at[n])

    def load_states(step):
        rows = pl.ds(pl.multiple_of(step * chunk, chunk), chunk)
        return load(states_hbm.at[rows], states.at[rows], 4 + step)

    loads = [
        load(attempts_hbm, attempts, 0),
        load(weight_hbm, weight, 1),
        load(theorem_hbm, theorem, 2),
        load(positive_hbm, positive, 3),
    ]
    loads[0].start()
    loads[1].start()
    for step in range(queries // chunk):
        load_states(step).start()
    loads[2].start()
    loads[3].start()

    greeted = [("blk", 1, n_blk), ("grp", 1, 2), ("grp", 2, n_grp // 2)]
    barrier = pltpu.get_barrier_semaphore()
    count = 0
    for axis, stride, size in greeted:
        for k in range(1, size):
            pl.semaphore_signal(
                barrier, inc=1, device_id=partner(axis, stride, size, k)[0], device_id_type=MESH
            )
            count += 1

    loads[0].wait()
    att = attempts[...].astype(jnp.float32)
    att_r = lax.rsqrt(jnp.mean(att * att, axis=1, keepdims=True) + epsilon)
    att_unit = att * att_r
    own_rows = pl.ds(pl.multiple_of(blk * own_att, own_att), own_att)
    panel[own_rows, :] = att_unit.astype(jnp.bfloat16)
    pl.semaphore_wait(barrier, count)
    gathers = [
        send(panel.at[own_rows], panel.at[own_rows], partner("blk", 1, n_blk, k)[0])
        for k in range(1, n_blk)
    ]

    loads[1].wait()
    weight_t[...] = weight[...].T

    def project(step, carry):
        load_states(step).wait()
        cols = pl.ds(pl.multiple_of(step * chunk, chunk), chunk)
        proj = lax.dot_general(
            weight_t[...], states[cols, :], NT, preferred_element_type=jnp.float32
        )
        r = lax.rsqrt(jnp.sum(proj * proj, axis=0, keepdims=True) * (1.0 / dim) + epsilon)
        inv_rms[:, cols] = r
        unit_t[:, cols] = (proj * r).astype(jnp.bfloat16)
        return carry

    lax.fori_loop(0, queries // chunk, project, 0)

    for copy in gathers:
        copy.wait_recv()
    loads[2].wait()
    loads[3].wait()
    panel_t[...] = panel[...].T
    theorem_col = jnp.broadcast_to(theorem[...].astype(jnp.float32), (8, n_att)).T[:, 0:1]

    def contrast(step, carry):
        cols = pl.ds(pl.multiple_of(step * chunk, chunk), chunk)
        unit = unit_t[:, cols]
        scores = jnp.dot(panel[...], unit, preferred_element_type=jnp.float32) * multiplier
        chosen = lax.broadcasted_iota(jnp.int32, scores.shape, 0) == positive[:, cols]
        label = jnp.sum(jnp.where(chosen, theorem_col, 0.0), axis=0, keepdims=True)
        expo = jnp.where(theorem_col == label, jnp.exp(scores), 0.0)
        total = jnp.sum(expo, axis=0, keepdims=True)
        pos_score = jnp.sum(jnp.where(chosen, scores, 0.0), axis=0, keepdims=True)
        loss[:, cols] = jnp.log(total) - pos_score
        w = (expo * (1.0 / total) - jnp.where(chosen, 1.0, 0.0)).astype(jnp.bfloat16)
        w_all[:, cols] = w
        along = jnp.sum(w.astype(jnp.float32) * scores, axis=0, keepdims=True) * (1.0 / dim)
        r = inv_rms[:, cols]
        g = jnp.dot(panel_t[...], w, preferred_element_type=jnp.float32)
        gproj_t[:, cols] = (
            g * (r * multiplier) - unit.astype(jnp.float32) * (r * along)
        ).astype(jnp.bfloat16)
        return carry

    lax.fori_loop(0, queries // chunk, contrast, 0)

    ga_t = lax.dot_general(unit_t[...], w_all[...], NT, preferred_element_type=jnp.float32)
    ga_stage[...] = (ga_t * multiplier).T.astype(jnp.bfloat16)
    ga_copies = []
    for k in range(1, n_blk):
        device, owner = partner("blk", 1, n_blk, k)
        rows = pl.ds(pl.multiple_of(owner * own_att, own_att), own_att)
        ga_copies.append(send(ga_stage.at[rows], ga_recv.at[k - 1], device))

    def weight_tile(which, part):
        rows = pl.ds(pl.multiple_of(which * half, half), half)
        tile = jnp.dot(
            gproj_t[rows, :], states[:, part * width:(part + 1) * width],
            preferred_element_type=jnp.float32,
        )
        return tile.T

    blocks = half // LANES
    bufs = [[None] * len(stages) for stages in plan]
    n = 0
    for part, stages in enumerate(plan):
        for j in range(len(stages)):
            bufs[part][j] = (stage_bufs[n], stage_bufs[n + 1])
            n += 2
    begin = [0] * PARTS
    pending = {}

    def start_stage(part, j):
        axis, stride, size, length, scatter = plan[part][j]
        stage, recv = bufs[part][j]
        here = member(axis, stride, size)
        now = begin[part]
        rows = pl.ds(pl.multiple_of(now, TILE), length)
        stage[...] = acc[part, rows, :].astype(jnp.bfloat16)
        copies = []
        for k in range(1, size):
            device, there = partner(axis, stride, size, k)
            if scatter:
                piece = length // size
                src = stage.at[pl.ds(pl.multiple_of(there * piece, TILE), piece)]
                copies.append(send(src, recv.at[k - 1], device))
            else:
                copies.append(send(stage, recv.at[here], device))
        pending[part, j] = copies

    def finish_stage(part, j):
        axis, stride, size, length, scatter = plan[part][j]
        stage, recv = bufs[part][j]
        here = member(axis, stride, size)
        for copy in pending[part, j]:
            copy.wait_recv()
        if scatter:
            piece = length // size
            begin[part] = begin[part] + here * piece
            rows = pl.ds(pl.multiple_of(begin[part], TILE), piece)
            total = acc[part, rows, :]
            for k in range(size - 1):
                total = total + recv[k].astype(jnp.float32)
        else:
            rows = pl.ds(pl.multiple_of(begin[part], TILE), length)
            recv[here] = stage[...]
            total = recv[0].astype(jnp.float32)
            for k in range(1, size):
                total = total + recv[k].astype(jnp.float32)
        acc[part, rows, :] = total

    sequence = (2, 0, 1)
    core_copies = {}
    for part in sequence:
        tile = weight_tile(1 - core, part)
        for e in range(blocks):
            core_send[part, e * width:(e + 1) * width, :] = (
                tile[:, e * LANES:(e + 1) * LANES].astype(jnp.bfloat16)
            )
        core_copies[part] = send(core_send.at[part], core_recv.at[part], {"blk": sibling})
    for part in sequence:
        tile = weight_tile(core, part)
        core_copies[part].wait_recv()
        for e in range(blocks):
            span = slice(e * width, (e + 1) * width)
            acc[part, span, :] = (
                tile[:, e * LANES:(e + 1) * LANES] + core_recv[part, span, :].astype(jnp.float32)
            )
        start_stage(part, 0)

    for copy in ga_copies:
        copy.wait_recv()
    ga = ga_stage[own_rows, :].astype(jnp.float32)
    for k in range(n_blk - 1):
        ga = ga + ga_recv[k].astype(jnp.float32)
    att = attempts[...].astype(jnp.float32)
    att_r = lax.rsqrt(jnp.mean(att * att, axis=1, keepdims=True) + epsilon)
    att_unit = att * att_r
    grad_att[...] = att_r * (ga - att_unit * jnp.mean(ga * att_unit, axis=1, keepdims=True))

    depth = len(plan[0])
    for j in range(depth):
        for part in sequence:
            finish_stage(part, j)
            if j + 1 < depth:
                start_stage(part, j + 1)

    where = {}
    for part in sequence:
        length = plan[part][0][3]
        for axis, stride, size, rows_in, scatter in plan[part]:
            length = rows_in // size if scatter else rows_in
        rows = pl.ds(pl.multiple_of(begin[part], TILE), length)
        res[core, part, rows, :] = acc[part, rows, :].astype(jnp.bfloat16)
        where[part] = begin[part]
    for j in reversed(range(depth)):
        for part in sequence:
            axis, stride, size, length, scatter = plan[part][j]
            if not scatter:
                continue
            piece = length // size
            rows = pl.ds(pl.multiple_of(where[part], TILE), piece)
            for later in range(j + 1, depth):
                for copy in pending.pop(("back", part, later), []):
                    copy.wait_recv()
            spot = res.at[core, part, rows]
            pending["back", part, j] = [
                send(spot, spot, partner(axis, stride, size, k)[0]) for k in range(1, size)
            ]
            where[part] = where[part] - member(axis, stride, size) * piece
    last = {}
    for part in sequence:
        for key in [key for key in pending if key[0] == "back" and key[1] == part]:
            for copy in pending.pop(key):
                copy.wait_recv()
        spot = res.at[core, part]
        last[part] = send(spot, spot, {"blk": sibling})

    def place(which, part):
        for e in range(blocks):
            cols = pl.ds(pl.multiple_of(which * half + e * LANES, LANES), LANES)
            grad_w[part * width:(part + 1) * width, cols] = (
                res[which, part, e * width:(e + 1) * width, :]
            )

    for part in sequence:
        place(core, part)
    for part in sequence:
        last[part].wait_recv()
        place(1 - core, part)
    for copy in started:
        copy.wait_send()


def write_out(loss, grad_att, grad_w, loss_hbm, grad_att_hbm, grad_w_hbm, wide, sems):
    copies = [
        pltpu.make_async_copy(loss, loss_hbm, sems.at[0]),
        pltpu.make_async_copy(grad_att, grad_att_hbm, sems.at[1]),
    ]
    for copy in copies:
        copy.start()
    step = wide.shape[0] // PARTS
    for part in range(PARTS):
        rows = pl.ds(part * step, step)
        wide[rows, :] = grad_w[rows, :].astype(jnp.float32)
        copy = pltpu.make_async_copy(wide.at[rows], grad_w_hbm.at[rows], sems.at[2 + part])
        copy.start()
        copies.append(copy)
    for copy in copies:
        copy.wait()


def on_device(n_grp, n_blk, states, query_weight, attempts, attempt_theorem, positive):
    queries, dim = states.shape
    own_att = attempts.shape[0]
    n_att = own_att * n_blk
    chunk = min(512, queries)
    rows = dim * (dim // 2) // PARTS // LANES
    plan = stage_plan(n_grp, n_blk, rows)
    copies = 2 * (n_blk - 1) + 2 * PARTS
    bf16, f32 = jnp.bfloat16, jnp.float32
    stage_bufs = []
    for stages in plan:
        for axis, stride, size, length, scatter in stages:
            copies += (size - 1) * (2 if scatter else 1)
            stage_bufs.append(pltpu.VMEM((length, LANES), bf16))
            if scatter:
                stage_bufs.append(pltpu.VMEM((size - 1, length // size, LANES), bf16))
            else:
                stage_bufs.append(pltpu.VMEM((size, length, LANES), bf16))
    vmem = pl.BlockSpec(memory_space=pltpu.VMEM)
    hbm = pl.BlockSpec(memory_space=pltpu.HBM)
    loss, grad_att, grad_w = pl.pallas_call(
        functools.partial(kernel, n_grp, n_blk, plan, chunk),
        out_shape=(
            jax.ShapeDtypeStruct((1, queries), f32),
            jax.ShapeDtypeStruct((own_att, dim), f32),
            jax.ShapeDtypeStruct((dim, dim), bf16),
        ),
        in_specs=[hbm] * 5,
        out_specs=(vmem,) * 3,
        scratch_shapes=[
            pltpu.VMEM((queries, dim), bf16),
            pltpu.VMEM((dim, dim), bf16),
            pltpu.VMEM((own_att, dim), bf16),
            pltpu.VMEM((1, n_att), jnp.int32),
            pltpu.VMEM((1, queries), jnp.int32),
            pltpu.SemaphoreType.DMA((4 + queries // chunk,)),
            pltpu.VMEM((dim, dim), bf16),
            pltpu.VMEM((dim, queries), bf16),
            pltpu.VMEM((dim, queries), bf16),
            pltpu.VMEM((n_att, queries), bf16),
            pltpu.VMEM((1, queries), f32),
            pltpu.VMEM((n_att, dim), bf16),
            pltpu.VMEM((dim, n_att), bf16),
            pltpu.VMEM((n_att, dim), bf16),
            pltpu.VMEM((n_blk - 1, own_att, dim), bf16),
            pltpu.VMEM((PARTS, rows, LANES), f32),
            pltpu.VMEM((PARTS, rows, LANES), bf16),
            pltpu.VMEM((PARTS, rows, LANES), bf16),
            pltpu.VMEM((2, PARTS, rows, LANES), bf16),
            pltpu.SemaphoreType.DMA((copies,)),
            pltpu.SemaphoreType.DMA((copies,)),
            *stage_bufs,
        ],
        compiler_params=pltpu.CompilerParams(
            collective_id=0, has_side_effects=True, vmem_limit_bytes=48 * 1024 * 1024
        ),
    )(*[pltpu.with_memory_space_constraint(x, pltpu.HBM) for x in (states, query_weight, attempts, attempt_theorem.reshape(1, n_att), positive.reshape(1, queries))])
    loss, grad_att, grad_w = pl.pallas_call(
        write_out,
        out_shape=(
            jax.ShapeDtypeStruct((1, queries), f32),
            jax.ShapeDtypeStruct((own_att, dim), f32),
            jax.ShapeDtypeStruct((dim, dim), f32),
        ),
        in_specs=[vmem] * 3,
        out_specs=(hbm,) * 3,
        scratch_shapes=[pltpu.VMEM((dim, dim), f32), pltpu.SemaphoreType.DMA((2 + PARTS,))],
        compiler_params=pltpu.CompilerParams(vmem_limit_bytes=8 * 1024 * 1024),
    )(loss, grad_att, grad_w)
    return loss.reshape(queries), grad_att, grad_w


def solution(mesh):
    n_grp, n_blk = mesh.shape["grp"], mesh.shape["blk"]
    in_specs = (P(("grp", "blk"), None), P(), P(("grp", "blk"), None), P("grp"), P(("grp", "blk")))
    out_specs = (P(("grp", "blk")), P(("grp", "blk"), None), P())
    return jax.shard_map(
        functools.partial(on_device, n_grp, n_blk),
        mesh=mesh, in_specs=in_specs, out_specs=out_specs, check_vma=False,
    )
```

```python
import functools

import jax
import jax.numpy as jnp
from jax import lax
from jax.experimental import pallas as pl
from jax.experimental.pallas import tpu as pltpu
from jax.sharding import PartitionSpec as P

logit_sharpness = 0.07
epsilon = 1e-06
MESH = pl.DeviceIdType.MESH
PARTS = 3
LANES = 128
TILE = 16
NT = (((1,), (1,)), ((), ()))


def stage_plan(n_grp, n_blk, units):
    along_x = ("blk", 2, n_blk // 2)
    along_y = ("grp", 1, 2)
    along_z = ("grp", 2, n_grp // 2)
    xyz, yxz, zxy = (along_x, along_y, along_z), (along_y, along_x, along_z), (along_z, along_x, along_y)
    pieces = []
    split = (((zxy, 1), (xyz, 1), (yxz, 1)), ((xyz, 2), (yxz, 1)), ((xyz, 1), (yxz, 2)))
    for block, row in enumerate(split):
        first = 0
        for order, count in row:
            rows = length = count * units
            stages = []
            for axis, stride, size in order:
                if size == 1:
                    continue
                scatter = length % (size * TILE) == 0
                stages.append((axis, stride, size, length, scatter))
                if scatter:
                    length //= size
            pieces.append((block, first, rows, stages))
            first += rows
    return pieces


def kernel(
    n_grp, n_blk, plan, chunk,
    states_hbm, weight_hbm, attempts_hbm, theorem_hbm, positive_hbm,
    loss, grad_att, res,
    states, weight, attempts, theorem, positive, load_sems,
    weight_t, unit_t, gproj_t, w_all, inv_rms, along_all, panel, panel_t,
    ga_stage, ga_core, ga_sum, ga_recv, acc, core_send, core_recv, send_sems, recv_sems, *stage_bufs,
):
    queries, dim = states.shape
    own_att = attempts.shape[0]
    n_att = own_att * n_blk
    half = dim // 2
    width = dim // PARTS
    multiplier = 1.0 / (logit_sharpness * dim)
    grp = lax.axis_index("grp")
    blk = lax.axis_index("blk")
    core = lax.rem(blk, 2)
    sibling = blk + 1 - 2 * core
    used = [0]
    started = []

    def member(axis, stride, size):
        index = grp if axis == "grp" else blk
        return lax.rem(index // stride, size)

    def partner(axis, stride, size, k):
        index = grp if axis == "grp" else blk
        here = lax.rem(index // stride, size)
        there = lax.rem(here + k, size)
        return {axis: index + (there - here) * stride}, there

    def send(src, dst, device):
        n = used[0]
        used[0] += 1
        copy = pltpu.make_async_remote_copy(
            src_ref=src, dst_ref=dst, send_sem=send_sems.at[n], recv_sem=recv_sems.at[n],
            device_id=device, device_id_type=MESH,
        )
        copy.start()
        started.append(copy)
        return copy

    def load(src, dst, n):
        return pltpu.make_async_copy(src, dst, load_sems.at[n])

    def load_states(step):
        rows = pl.ds(pl.multiple_of(step * chunk, chunk), chunk)
        return load(states_hbm.at[rows], states.at[rows], 4 + step)

    loads = [
        load(attempts_hbm, attempts, 0),
        load(weight_hbm, weight, 1),
        load(theorem_hbm, theorem, 2),
        load(positive_hbm, positive, 3),
    ]
    loads[0].start()
    loads[1].start()
    for step in range(queries // chunk):
        load_states(step).start()
    loads[2].start()
    loads[3].start()

    greeted = [("blk", 1, n_blk), ("grp", 1, 2), ("grp", 2, n_grp // 2)]
    barrier = pltpu.get_barrier_semaphore()
    count = 0
    for axis, stride, size in greeted:
        for k in range(1, size):
            pl.semaphore_signal(
                barrier, inc=1, device_id=partner(axis, stride, size, k)[0], device_id_type=MESH
            )
            count += 1

    loads[0].wait()
    att = attempts[...].astype(jnp.float32)
    att_r = lax.rsqrt(jnp.mean(att * att, axis=1, keepdims=True) + epsilon)
    att_unit = att * att_r
    own_rows = pl.ds(pl.multiple_of(blk * own_att, own_att), own_att)
    panel[own_rows, :] = att_unit.astype(jnp.bfloat16)
    pl.semaphore_wait(barrier, count)
    across = [
        send(panel.at[own_rows], panel.at[own_rows], partner("blk", 2, n_blk // 2, k)[0])
        for k in range(1, n_blk // 2)
    ]
    to_sibling = [send(panel.at[own_rows], panel.at[own_rows], {"blk": sibling})]

    loads[1].wait()
    weight_t[...] = weight[...].T

    def project(step, carry):
        load_states(step).wait()
        cols = pl.ds(pl.multiple_of(step * chunk, chunk), chunk)
        proj = lax.dot_general(
            weight_t[...], states[cols, :], NT, preferred_element_type=jnp.float32
        )
        r = lax.rsqrt(jnp.sum(proj * proj, axis=0, keepdims=True) * (1.0 / dim) + epsilon)
        inv_rms[:, cols] = r
        unit_t[:, cols] = (proj * r).astype(jnp.bfloat16)
        return carry

    steps = queries // chunk
    lax.fori_loop(0, steps // 2, project, 0)
    for k, copy in enumerate(across):
        copy.wait_recv()
        source = lax.rem(blk // 2 + n_blk // 2 - (k + 1), n_blk // 2) * 2 + core
        rows = pl.ds(pl.multiple_of(source * own_att, own_att), own_att)
        to_sibling.append(send(panel.at[rows], panel.at[rows], {"blk": sibling}))
    lax.fori_loop(steps // 2, steps, project, 0)

    for copy in to_sibling:
        copy.wait_recv()
    loads[2].wait()
    loads[3].wait()
    panel_t[...] = panel[...].T
    theorem_col = jnp.broadcast_to(theorem[...].astype(jnp.float32), (8, n_att)).T[:, 0:1]

    def contrast(step, carry):
        cols = pl.ds(pl.multiple_of(step * chunk, chunk), chunk)
        unit = unit_t[:, cols]
        scores = jnp.dot(panel[...], unit, preferred_element_type=jnp.float32) * multiplier
        chosen = lax.broadcasted_iota(jnp.int32, scores.shape, 0) == positive[:, cols]
        label = jnp.sum(jnp.where(chosen, theorem_col, 0.0), axis=0, keepdims=True)
        expo = jnp.where(theorem_col == label, jnp.exp(scores), 0.0)
        total = jnp.sum(expo, axis=0, keepdims=True)
        pos_score = jnp.sum(jnp.where(chosen, scores, 0.0), axis=0, keepdims=True)
        loss[:, cols] = jnp.log(total) - pos_score
        w = (expo * (1.0 / total) - jnp.where(chosen, 1.0, 0.0)).astype(jnp.bfloat16)
        w_all[:, cols] = w
        along = jnp.sum(w.astype(jnp.float32) * scores, axis=0, keepdims=True) * (1.0 / dim)
        along_all[:, cols] = along * inv_rms[:, cols]
        return carry

    lax.fori_loop(0, steps, contrast, 0)

    begin = [first for block, first, rows, stages in plan]
    pending = [None] * len(plan)
    bufs, n = [], 0
    for block, first, rows, stages in plan:
        bufs.append([(stage_bufs[n + 2 * j], stage_bufs[n + 2 * j + 1]) for j in range(len(stages))])
        n += 2 * len(stages)

    def start_stage(piece, j):
        block = plan[piece][0]
        axis, stride, size, length, scatter = plan[piece][3][j]
        stage, recv = bufs[piece][j]
        here = member(axis, stride, size)
        rows = pl.ds(pl.multiple_of(begin[piece], TILE), length)
        stage[...] = acc[block, rows, :].astype(jnp.bfloat16)
        pending[piece] = []
        for k in range(1, size):
            device, there = partner(axis, stride, size, k)
            if scatter:
                part = length // size
                src = stage.at[pl.ds(pl.multiple_of(there * part, TILE), part)]
                pending[piece].append(send(src, recv.at[k - 1], device))
            else:
                pending[piece].append(send(stage, recv.at[here], device))

    def finish_stage(piece, j):
        block = plan[piece][0]
        axis, stride, size, length, scatter = plan[piece][3][j]
        stage, recv = bufs[piece][j]
        here = member(axis, stride, size)
        for copy in pending[piece]:
            copy.wait_recv()
        if scatter:
            part = length // size
            begin[piece] = begin[piece] + here * part
            rows = pl.ds(pl.multiple_of(begin[piece], TILE), part)
            total = acc[block, rows, :]
            for k in range(size - 1):
                total = total + recv[k].astype(jnp.float32)
        else:
            rows = pl.ds(pl.multiple_of(begin[piece], TILE), length)
            recv[here] = stage[...]
            total = recv[0].astype(jnp.float32)
            for k in range(1, size):
                total = total + recv[k].astype(jnp.float32)
        if j + 1 < len(plan[piece][3]):
            acc[block, rows, :] = total
        else:
            res[core, block, rows, :] = total.astype(jnp.bfloat16)

    def start_back(piece, j):
        block = plan[piece][0]
        axis, stride, size, length, scatter = plan[piece][3][j]
        part = length // size
        rows = pl.ds(pl.multiple_of(begin[piece], TILE), part)
        spot = res.at[core, block, rows]
        pending[piece] = [
            send(spot, spot, partner(axis, stride, size, k)[0]) for k in range(1, size)
        ]
        begin[piece] = begin[piece] - member(axis, stride, size) * part

    def steps_of(piece):
        block, first, rows, stages = plan[piece]
        start_stage(piece, 0)
        yield
        for j in range(len(stages)):
            finish_stage(piece, j)
            if j + 1 < len(stages):
                start_stage(piece, j + 1)
                yield
        for j in reversed(range(len(stages))):
            if stages[j][4]:
                start_back(piece, j)
                yield
                for copy in pending[piece]:
                    copy.wait_recv()
        spot = res.at[core, block, pl.ds(first, rows)]
        pending[piece] = [send(spot, spot, {"blk": sibling})]
        yield
        pending[piece][0].wait_recv()

    runs = [steps_of(piece) for piece in range(len(plan))]

    def advance(block):
        more = False
        for piece in range(len(plan)):
            if plan[piece][0] == block:
                more = next(runs[piece], "end") != "end" or more
        return more

    slabs = width // LANES
    subs = half // LANES
    core_copies = []

    def grad_proj_third(block):
        rows = slice(block * width, (block + 1) * width)
        g = jnp.dot(panel_t[rows, :], w_all[...], preferred_element_type=jnp.float32)
        gproj_t[rows, :] = (
            g * (inv_rms[...] * multiplier) - unit_t[rows, :].astype(jnp.float32) * along_all[...]
        ).astype(jnp.bfloat16)

    def weight_third(block):
        rows = slice(block * width, (block + 1) * width)
        for which, keep in ((1 - core, False), (core, True)):
            cols = pl.ds(pl.multiple_of(which * half, half), half)
            tile = jnp.dot(
                gproj_t[rows, :], states[:, cols], preferred_element_type=jnp.float32
            ).T
            for u in range(subs):
                for e in range(slabs):
                    at = slice((u * slabs + e) * LANES, (u * slabs + e + 1) * LANES)
                    value = tile[u * LANES:(u + 1) * LANES, e * LANES:(e + 1) * LANES]
                    if keep:
                        acc[block, at, :] = value
                    else:
                        core_send[block, at, :] = value.astype(jnp.bfloat16)
            if not keep:
                core_copies.append(send(core_send.at[block], core_recv.at[block], {"blk": sibling}))

    def add_sibling(block):
        core_copies[block].wait_recv()
        acc[block] += core_recv[block].astype(jnp.float32)

    for block in range(PARTS):
        grad_proj_third(block)
        if block >= 1:
            add_sibling(block - 1)
            advance(block - 1)
        weight_third(block)

    advance(0)
    ga = lax.dot_general(unit_t[...], w_all[...], NT, preferred_element_type=jnp.float32)
    ga = (ga * multiplier).T.astype(jnp.bfloat16)
    for owner in range(n_blk):
        ga_stage[owner % 2, owner // 2] = ga[owner * own_att:(owner + 1) * own_att, :]
    ga_copy = send(ga_stage.at[1 - core], ga_core, {"blk": sibling})
    add_sibling(PARTS - 1)
    advance(PARTS - 1)
    advance(1)
    advance(0)
    advance(2)
    advance(1)
    advance(0)

    ga_copy.wait_recv()
    ga_sum[...] = (
        ga_stage[core].astype(jnp.float32) + ga_core[...].astype(jnp.float32)
    ).astype(jnp.bfloat16)
    ga_copies = []
    for k in range(1, n_blk // 2):
        device, owner = partner("blk", 2, n_blk // 2, k)
        ga_copies.append(send(ga_sum.at[owner], ga_recv.at[k - 1], device))

    advance(2)
    advance(1)
    advance(0)
    advance(2)
    advance(1)
    advance(0)
    for copy in ga_copies:
        copy.wait_recv()
    ga = ga_stage[core, blk // 2].astype(jnp.float32) + ga_core[blk // 2].astype(jnp.float32)
    for k in range(n_blk // 2 - 1):
        ga = ga + ga_recv[k].astype(jnp.float32)
    att = attempts[...].astype(jnp.float32)
    att_r = lax.rsqrt(jnp.mean(att * att, axis=1, keepdims=True) + epsilon)
    att_unit = att * att_r
    grad_att[...] = att_r * (ga - att_unit * jnp.mean(ga * att_unit, axis=1, keepdims=True))

    more = True
    while more:
        more = any([advance(block) for block in (2, 1, 0)])
    for copy in started:
        copy.wait_send()


def write_out(loss, grad_att, res, loss_hbm, grad_att_hbm, grad_w_hbm, wide, sems):
    copies = [
        pltpu.make_async_copy(loss, loss_hbm, sems.at[0]),
        pltpu.make_async_copy(grad_att, grad_att_hbm, sems.at[1]),
    ]
    for copy in copies:
        copy.start()
    dim = wide.shape[0]
    half, width = dim // 2, dim // PARTS
    slabs, subs = width // LANES, half // LANES
    for which in range(2):
        for u in range(subs):
            row = which * half + u * LANES
            for block in range(PARTS):
                for e in range(slabs):
                    at = (u * slabs + e) * LANES
                    col = block * width + e * LANES
                    wide[row:row + LANES, col:col + LANES] = (
                        res[which, block, at:at + LANES, :].astype(jnp.float32)
                    )
            rows = pl.ds(row, LANES)
            copy = pltpu.make_async_copy(
                wide.at[rows], grad_w_hbm.at[rows], sems.at[2 + which * subs + u]
            )
            copy.start()
            copies.append(copy)
    for copy in copies:
        copy.wait()


def on_device(n_grp, n_blk, states, query_weight, attempts, attempt_theorem, positive):
    queries, dim = states.shape
    own_att = attempts.shape[0]
    n_att = own_att * n_blk
    chunk = min(512, queries)
    rows = dim * (dim // 2) // PARTS // LANES
    plan = stage_plan(n_grp, n_blk, rows // 3)
    copies = 2 * n_blk + 2 * PARTS + len(plan)
    bf16, f32 = jnp.bfloat16, jnp.float32
    stage_bufs = []
    for block, first, count, stages in plan:
        for axis, stride, size, length, scatter in stages:
            copies += (size - 1) * (2 if scatter else 1)
            stage_bufs.append(pltpu.VMEM((length, LANES), bf16))
            if scatter:
                stage_bufs.append(pltpu.VMEM((size - 1, length // size, LANES), bf16))
            else:
                stage_bufs.append(pltpu.VMEM((size, length, LANES), bf16))
    vmem = pl.BlockSpec(memory_space=pltpu.VMEM)
    hbm = pl.BlockSpec(memory_space=pltpu.HBM)
    loss, grad_att, res = pl.pallas_call(
        functools.partial(kernel, n_grp, n_blk, plan, chunk),
        out_shape=(
            jax.ShapeDtypeStruct((1, queries), f32),
            jax.ShapeDtypeStruct((own_att, dim), f32),
            jax.ShapeDtypeStruct((2, PARTS, rows, LANES), bf16),
        ),
        in_specs=[hbm] * 5,
        out_specs=(vmem,) * 3,
        scratch_shapes=[
            pltpu.VMEM((queries, dim), bf16),
            pltpu.VMEM((dim, dim), bf16),
            pltpu.VMEM((own_att, dim), bf16),
            pltpu.VMEM((1, n_att), jnp.int32),
            pltpu.VMEM((1, queries), jnp.int32),
            pltpu.SemaphoreType.DMA((4 + queries // chunk,)),
            pltpu.VMEM((dim, dim), bf16),
            pltpu.VMEM((dim, queries), bf16),
            pltpu.VMEM((dim, queries), bf16),
            pltpu.VMEM((n_att, queries), bf16),
            pltpu.VMEM((1, queries), f32),
            pltpu.VMEM((1, queries), f32),
            pltpu.VMEM((n_att, dim), bf16),
            pltpu.VMEM((dim, n_att), bf16),
            pltpu.VMEM((2, n_blk // 2, own_att, dim), bf16),
            pltpu.VMEM((n_blk // 2, own_att, dim), bf16),
            pltpu.VMEM((n_blk // 2, own_att, dim), bf16),
            pltpu.VMEM((max(n_blk // 2 - 1, 1), own_att, dim), bf16),
            pltpu.VMEM((PARTS, rows, LANES), f32),
            pltpu.VMEM((PARTS, rows, LANES), bf16),
            pltpu.VMEM((PARTS, rows, LANES), bf16),
            pltpu.SemaphoreType.DMA((copies,)),
            pltpu.SemaphoreType.DMA((copies,)),
            *stage_bufs,
        ],
        compiler_params=pltpu.CompilerParams(
            collective_id=0, has_side_effects=True, vmem_limit_bytes=48 * 1024 * 1024
        ),
    )(*[pltpu.with_memory_space_constraint(x, pltpu.HBM) for x in (states, query_weight, attempts, attempt_theorem.reshape(1, n_att), positive.reshape(1, queries))])
    loss, grad_att, grad_w = pl.pallas_call(
        write_out,
        out_shape=(
            jax.ShapeDtypeStruct((1, queries), f32),
            jax.ShapeDtypeStruct((own_att, dim), f32),
            jax.ShapeDtypeStruct((dim, dim), f32),
        ),
        in_specs=[vmem] * 3,
        out_specs=(hbm,) * 3,
        scratch_shapes=[pltpu.VMEM((dim, dim), f32), pltpu.SemaphoreType.DMA((2 + dim // LANES,))],
        compiler_params=pltpu.CompilerParams(vmem_limit_bytes=8 * 1024 * 1024),
    )(loss, grad_att, res)
    return loss.reshape(queries), grad_att, grad_w


def solution(mesh):
    n_grp, n_blk = mesh.shape["grp"], mesh.shape["blk"]
    in_specs = (P(("grp", "blk"), None), P(), P(("grp", "blk"), None), P("grp"), P(("grp", "blk")))
    out_specs = (P(("grp", "blk")), P(("grp", "blk"), None), P())
    return jax.shard_map(
        functools.partial(on_device, n_grp, n_blk),
        mesh=mesh, in_specs=in_specs, out_specs=out_specs, check_vma=False,
    )
```

```python
import functools

import jax
import jax.numpy as jnp
from jax import lax
from jax.experimental import pallas as pl
from jax.experimental.pallas import tpu as pltpu
from jax.sharding import PartitionSpec as P

logit_sharpness = 0.07
epsilon = 1e-06
MESH = pl.DeviceIdType.MESH
PARTS = 3
LANES = 128
TILE = 16
NT = (((1,), (1,)), ((), ()))


def stage_plan(n_grp, n_blk, units):
    along_x = ("blk", 2, n_blk // 2)
    along_y = ("grp", 1, 2)
    along_z = ("grp", 2, n_grp // 2)
    xyz, yxz, zxy = (along_x, along_y, along_z), (along_y, along_x, along_z), (along_z, along_x, along_y)
    pieces = []
    split = (((zxy, 1), (xyz, 1), (yxz, 1)), ((xyz, 2), (yxz, 1)), ((xyz, 1), (yxz, 2)))
    for block, row in enumerate(split):
        first = 0
        for order, count in row:
            rows = length = count * units
            stages = []
            for axis, stride, size in order:
                if size == 1:
                    continue
                scatter = length % (size * TILE) == 0
                stages.append((axis, stride, size, length, scatter))
                if scatter:
                    length //= size
            pieces.append((block, first, rows, stages))
            first += rows
    return pieces


def kernel(
    n_grp, n_blk, plan, chunk,
    states_hbm, weight_hbm, attempts_hbm, theorem_hbm, positive_hbm,
    loss, grad_att, res,
    states, weight, attempts, theorem, positive, load_sems,
    weight_t, unit_t, gproj_t, w_all, inv_rms, panel, panel_t,
    ga_stage, ga_core, ga_sum, ga_recv, acc, core_send, core_recv, send_sems, recv_sems, *stage_bufs,
):
    queries, dim = states.shape
    own_att = attempts.shape[0]
    n_att = own_att * n_blk
    half = dim // 2
    width = dim // PARTS
    multiplier = 1.0 / (logit_sharpness * dim)
    grp = lax.axis_index("grp")
    blk = lax.axis_index("blk")
    core = lax.rem(blk, 2)
    sibling = blk + 1 - 2 * core
    used = [0]
    started = []

    def member(axis, stride, size):
        index = grp if axis == "grp" else blk
        return lax.rem(index // stride, size)

    def partner(axis, stride, size, k):
        index = grp if axis == "grp" else blk
        here = lax.rem(index // stride, size)
        there = lax.rem(here + k, size)
        return {axis: index + (there - here) * stride}, there

    def send(src, dst, device):
        n = used[0]
        used[0] += 1
        copy = pltpu.make_async_remote_copy(
            src_ref=src, dst_ref=dst, send_sem=send_sems.at[n], recv_sem=recv_sems.at[n],
            device_id=device, device_id_type=MESH,
        )
        copy.start()
        started.append(copy)
        return copy

    def load(src, dst, n):
        return pltpu.make_async_copy(src, dst, load_sems.at[n])

    def load_states(step):
        rows = pl.ds(pl.multiple_of(step * chunk, chunk), chunk)
        return load(states_hbm.at[rows], states.at[rows], 4 + step)

    loads = [
        load(attempts_hbm, attempts, 0),
        load(weight_hbm, weight, 1),
        load(theorem_hbm, theorem, 2),
        load(positive_hbm, positive, 3),
    ]
    loads[0].start()
    loads[1].start()
    for step in range(queries // chunk):
        load_states(step).start()
    loads[2].start()
    loads[3].start()

    greeted = [("blk", 1, n_blk), ("grp", 1, 2), ("grp", 2, n_grp // 2)]
    barrier = pltpu.get_barrier_semaphore()
    count = 0
    for axis, stride, size in greeted:
        for k in range(1, size):
            pl.semaphore_signal(
                barrier, inc=1, device_id=partner(axis, stride, size, k)[0], device_id_type=MESH
            )
            count += 1

    loads[0].wait()
    att = attempts[...].astype(jnp.float32)
    att_r = lax.rsqrt(jnp.mean(att * att, axis=1, keepdims=True) + epsilon)
    att_unit = att * att_r
    own_rows = pl.ds(pl.multiple_of(blk * own_att, own_att), own_att)
    panel[own_rows, :] = att_unit.astype(jnp.bfloat16)
    pl.semaphore_wait(barrier, count)
    across = [
        send(panel.at[own_rows], panel.at[own_rows], partner("blk", 2, n_blk // 2, k)[0])
        for k in range(1, n_blk // 2)
    ]
    to_sibling = [send(panel.at[own_rows], panel.at[own_rows], {"blk": sibling})]

    loads[1].wait()
    weight_t[...] = weight[...].T

    def project(step):
        load_states(step).wait()
        cols = pl.ds(step * chunk, chunk)
        proj = lax.dot_general(
            weight_t[...], states[cols, :], NT, preferred_element_type=jnp.float32
        )
        r = lax.rsqrt(jnp.sum(proj * proj, axis=0, keepdims=True) * (1.0 / dim) + epsilon)
        inv_rms[:, cols] = r
        unit_t[:, cols] = (proj * r).astype(jnp.bfloat16)

    steps = queries // chunk
    for step in range(steps // 2):
        project(step)
    for k, copy in enumerate(across):
        copy.wait_recv()
        source = lax.rem(blk // 2 + n_blk // 2 - (k + 1), n_blk // 2) * 2 + core
        rows = pl.ds(pl.multiple_of(source * own_att, own_att), own_att)
        to_sibling.append(send(panel.at[rows], panel.at[rows], {"blk": sibling}))
    for step in range(steps // 2, steps):
        project(step)

    for copy in to_sibling:
        copy.wait_recv()
    loads[2].wait()
    loads[3].wait()
    panel_t[...] = panel[...].T
    theorem_col = jnp.broadcast_to(theorem[...].astype(jnp.float32), (8, n_att)).T[:, 0:1]

    def contrast(step):
        cols = pl.ds(step * chunk, chunk)
        unit = unit_t[:, cols]
        scores = jnp.dot(panel[...], unit, preferred_element_type=jnp.float32) * multiplier
        chosen = lax.broadcasted_iota(jnp.int32, scores.shape, 0) == positive[:, cols]
        label = jnp.sum(jnp.where(chosen, theorem_col, 0.0), axis=0, keepdims=True)
        expo = jnp.where(theorem_col == label, jnp.exp(scores), 0.0)
        total = jnp.sum(expo, axis=0, keepdims=True)
        pos_score = jnp.sum(jnp.where(chosen, scores, 0.0), axis=0, keepdims=True)
        loss[:, cols] = jnp.log(total) - pos_score
        w = (expo * (1.0 / total) - jnp.where(chosen, 1.0, 0.0)).astype(jnp.bfloat16)
        w_all[:, cols] = w
        along = jnp.sum(w.astype(jnp.float32) * scores, axis=0, keepdims=True) * (1.0 / dim)
        r = inv_rms[:, cols]
        g = jnp.dot(panel_t[...], w, preferred_element_type=jnp.float32)
        gproj_t[:, cols] = (
            g * (r * multiplier) - unit.astype(jnp.float32) * (r * along)
        ).astype(jnp.bfloat16)

    for step in range(steps):
        contrast(step)

    begin = [first for block, first, rows, stages in plan]
    pending = [None] * len(plan)
    bufs, n = [], 0
    for block, first, rows, stages in plan:
        bufs.append([(stage_bufs[n + 2 * j], stage_bufs[n + 2 * j + 1]) for j in range(len(stages))])
        n += 2 * len(stages)

    def start_stage(piece, j):
        block = plan[piece][0]
        axis, stride, size, length, scatter = plan[piece][3][j]
        stage, recv = bufs[piece][j]
        here = member(axis, stride, size)
        rows = pl.ds(pl.multiple_of(begin[piece], TILE), length)
        stage[...] = acc[block, core, rows, :].astype(jnp.bfloat16)
        pending[piece] = []
        for k in range(1, size):
            device, there = partner(axis, stride, size, k)
            if scatter:
                part = length // size
                src = stage.at[pl.ds(pl.multiple_of(there * part, TILE), part)]
                pending[piece].append(send(src, recv.at[k - 1], device))
            else:
                pending[piece].append(send(stage, recv.at[here], device))

    def finish_stage(piece, j):
        block = plan[piece][0]
        axis, stride, size, length, scatter = plan[piece][3][j]
        stage, recv = bufs[piece][j]
        here = member(axis, stride, size)
        for copy in pending[piece]:
            copy.wait_recv()
        if scatter:
            part = length // size
            begin[piece] = begin[piece] + here * part
            rows = pl.ds(pl.multiple_of(begin[piece], TILE), part)
            total = acc[block, core, rows, :]
            for k in range(size - 1):
                total = total + recv[k].astype(jnp.float32)
        else:
            rows = pl.ds(pl.multiple_of(begin[piece], TILE), length)
            recv[here] = stage[...]
            total = recv[0].astype(jnp.float32)
            for k in range(1, size):
                total = total + recv[k].astype(jnp.float32)
        if j + 1 < len(plan[piece][3]):
            acc[block, core, rows, :] = total
        else:
            res[core, block, rows, :] = total.astype(jnp.bfloat16)

    def start_back(piece, j):
        block = plan[piece][0]
        axis, stride, size, length, scatter = plan[piece][3][j]
        part = length // size
        rows = pl.ds(pl.multiple_of(begin[piece], TILE), part)
        spot = res.at[core, block, rows]
        pending[piece] = [
            send(spot, spot, partner(axis, stride, size, k)[0]) for k in range(1, size)
        ]
        begin[piece] = begin[piece] - member(axis, stride, size) * part

    def steps_of(piece):
        block, first, rows, stages = plan[piece]
        start_stage(piece, 0)
        yield
        for j in range(len(stages)):
            finish_stage(piece, j)
            if j + 1 < len(stages):
                start_stage(piece, j + 1)
                yield
        for j in reversed(range(len(stages))):
            if stages[j][4]:
                start_back(piece, j)
                yield
                for copy in pending[piece]:
                    copy.wait_recv()
        spot = res.at[core, block, pl.ds(first, rows)]
        pending[piece] = [send(spot, spot, {"blk": sibling})]
        yield
        pending[piece][0].wait_recv()

    runs = [steps_of(piece) for piece in range(len(plan))]

    def advance(block):
        more = False
        for piece in range(len(plan)):
            if plan[piece][0] == block:
                more = next(runs[piece], "end") != "end" or more
        return more

    slabs = half // LANES
    core_copies = []

    def weight_third(block):
        tile = jnp.dot(
            gproj_t[...], states[:, block * width:(block + 1) * width],
            preferred_element_type=jnp.float32,
        ).T
        for which in range(2):
            for e in range(slabs):
                col = which * half + e * LANES
                acc[block, which, e * width:(e + 1) * width, :] = tile[:, col:col + LANES]
        core_send[block] = acc[block, 1 - core].astype(jnp.bfloat16)
        core_copies.append(send(core_send.at[block], core_recv.at[block], {"blk": sibling}))

    def add_sibling(block):
        core_copies[block].wait_recv()
        acc[block, core] += core_recv[block].astype(jnp.float32)

    for block in range(PARTS):
        weight_third(block)
        if block >= 1:
            add_sibling(block - 1)
            advance(block - 1)

    advance(0)
    ga = lax.dot_general(unit_t[...], w_all[...], NT, preferred_element_type=jnp.float32)
    ga = (ga * multiplier).T.astype(jnp.bfloat16)
    for owner in range(n_blk):
        ga_stage[owner % 2, owner // 2] = ga[owner * own_att:(owner + 1) * own_att, :]
    ga_copy = send(ga_stage.at[1 - core], ga_core, {"blk": sibling})
    add_sibling(PARTS - 1)
    advance(PARTS - 1)
    advance(1)
    advance(0)
    advance(2)
    advance(1)
    advance(0)

    ga_copy.wait_recv()
    ga_sum[...] = (
        ga_stage[core].astype(jnp.float32) + ga_core[...].astype(jnp.float32)
    ).astype(jnp.bfloat16)
    ga_copies = []
    for k in range(1, n_blk // 2):
        device, owner = partner("blk", 2, n_blk // 2, k)
        ga_copies.append(send(ga_sum.at[owner], ga_recv.at[k - 1], device))

    advance(2)
    advance(1)
    advance(0)
    advance(2)
    advance(1)
    advance(0)
    for copy in ga_copies:
        copy.wait_recv()
    ga = ga_stage[core, blk // 2].astype(jnp.float32) + ga_core[blk // 2].astype(jnp.float32)
    for k in range(n_blk // 2 - 1):
        ga = ga + ga_recv[k].astype(jnp.float32)
    att = attempts[...].astype(jnp.float32)
    att_r = lax.rsqrt(jnp.mean(att * att, axis=1, keepdims=True) + epsilon)
    att_unit = att * att_r
    grad_att[...] = att_r * (ga - att_unit * jnp.mean(ga * att_unit, axis=1, keepdims=True))

    more = True
    while more:
        more = any([advance(block) for block in (2, 1, 0)])
    for copy in started:
        copy.wait_send()


def write_out(loss, grad_att, res, loss_hbm, grad_att_hbm, grad_w_hbm, wide, sems):
    copies = [
        pltpu.make_async_copy(loss, loss_hbm, sems.at[0]),
        pltpu.make_async_copy(grad_att, grad_att_hbm, sems.at[1]),
    ]
    for copy in copies:
        copy.start()
    dim = wide.shape[0]
    half, width = dim // 2, dim // PARTS
    slabs = half // LANES
    for block in range(PARTS):
        rows = pl.ds(block * width, width)
        for which in range(2):
            for e in range(slabs):
                col = which * half + e * LANES
                wide[rows, col:col + LANES] = (
                    res[which, block, e * width:(e + 1) * width, :].astype(jnp.float32)
                )
        copy = pltpu.make_async_copy(wide.at[rows], grad_w_hbm.at[rows], sems.at[2 + block])
        copy.start()
        copies.append(copy)
    for copy in copies:
        copy.wait()


def on_device(n_grp, n_blk, states, query_weight, attempts, attempt_theorem, positive):
    queries, dim = states.shape
    own_att = attempts.shape[0]
    n_att = own_att * n_blk
    chunk = min(512, queries)
    rows = dim * (dim // 2) // PARTS // LANES
    plan = stage_plan(n_grp, n_blk, rows // 3)
    copies = 2 * n_blk + 2 * PARTS + len(plan)
    bf16, f32 = jnp.bfloat16, jnp.float32
    stage_bufs = []
    for block, first, count, stages in plan:
        for axis, stride, size, length, scatter in stages:
            copies += (size - 1) * (2 if scatter else 1)
            stage_bufs.append(pltpu.VMEM((length, LANES), bf16))
            if scatter:
                stage_bufs.append(pltpu.VMEM((size - 1, length // size, LANES), bf16))
            else:
                stage_bufs.append(pltpu.VMEM((size, length, LANES), bf16))
    vmem = pl.BlockSpec(memory_space=pltpu.VMEM)
    hbm = pl.BlockSpec(memory_space=pltpu.HBM)
    loss, grad_att, res = pl.pallas_call(
        functools.partial(kernel, n_grp, n_blk, plan, chunk),
        out_shape=(
            jax.ShapeDtypeStruct((1, queries), f32),
            jax.ShapeDtypeStruct((own_att, dim), f32),
            jax.ShapeDtypeStruct((2, PARTS, rows, LANES), bf16),
        ),
        in_specs=[hbm] * 5,
        out_specs=(vmem,) * 3,
        scratch_shapes=[
            pltpu.VMEM((queries, dim), bf16),
            pltpu.VMEM((dim, dim), bf16),
            pltpu.VMEM((own_att, dim), bf16),
            pltpu.VMEM((1, n_att), jnp.int32),
            pltpu.VMEM((1, queries), jnp.int32),
            pltpu.SemaphoreType.DMA((4 + queries // chunk,)),
            pltpu.VMEM((dim, dim), bf16),
            pltpu.VMEM((dim, queries), bf16),
            pltpu.VMEM((dim, queries), bf16),
            pltpu.VMEM((n_att, queries), bf16),
            pltpu.VMEM((1, queries), f32),
            pltpu.VMEM((n_att, dim), bf16),
            pltpu.VMEM((dim, n_att), bf16),
            pltpu.VMEM((2, n_blk // 2, own_att, dim), bf16),
            pltpu.VMEM((n_blk // 2, own_att, dim), bf16),
            pltpu.VMEM((n_blk // 2, own_att, dim), bf16),
            pltpu.VMEM((max(n_blk // 2 - 1, 1), own_att, dim), bf16),
            pltpu.VMEM((PARTS, 2, rows, LANES), f32),
            pltpu.VMEM((PARTS, rows, LANES), bf16),
            pltpu.VMEM((PARTS, rows, LANES), bf16),
            pltpu.SemaphoreType.DMA((copies,)),
            pltpu.SemaphoreType.DMA((copies,)),
            *stage_bufs,
        ],
        compiler_params=pltpu.CompilerParams(
            collective_id=0, has_side_effects=True, vmem_limit_bytes=48 * 1024 * 1024
        ),
    )(*[pltpu.with_memory_space_constraint(x, pltpu.HBM) for x in (states, query_weight, attempts, attempt_theorem.reshape(1, n_att), positive.reshape(1, queries))])
    loss, grad_att, grad_w = pl.pallas_call(
        write_out,
        out_shape=(
            jax.ShapeDtypeStruct((1, queries), f32),
            jax.ShapeDtypeStruct((own_att, dim), f32),
            jax.ShapeDtypeStruct((dim, dim), f32),
        ),
        in_specs=[vmem] * 3,
        out_specs=(hbm,) * 3,
        scratch_shapes=[pltpu.VMEM((dim, dim), f32), pltpu.SemaphoreType.DMA((2 + PARTS,))],
        compiler_params=pltpu.CompilerParams(vmem_limit_bytes=8 * 1024 * 1024),
    )(loss, grad_att, res)
    return loss.reshape(queries), grad_att, grad_w


def solution(mesh):
    n_grp, n_blk = mesh.shape["grp"], mesh.shape["blk"]
    in_specs = (P(("grp", "blk"), None), P(), P(("grp", "blk"), None), P("grp"), P(("grp", "blk")))
    out_specs = (P(("grp", "blk")), P(("grp", "blk"), None), P())
    return jax.shard_map(
        functools.partial(on_device, n_grp, n_blk),
        mesh=mesh, in_specs=in_specs, out_specs=out_specs, check_vma=False,
    )
```

```python
import functools

import jax
import jax.numpy as jnp
from jax import lax
from jax.experimental import pallas as pl
from jax.experimental.pallas import tpu as pltpu
from jax.sharding import PartitionSpec as P

logit_sharpness = 0.07
epsilon = 1e-06
MESH = pl.DeviceIdType.MESH
PARTS = 3
LANES = 128
TILE = 16
NT = (((1,), (1,)), ((), ()))


def stage_plan(n_grp, n_blk, units):
    along_x = ("blk", 2, n_blk // 2)
    along_y = ("grp", 1, 2)
    along_z = ("grp", 2, n_grp // 2)
    xyz, yxz, zxy = (along_x, along_y, along_z), (along_y, along_x, along_z), (along_z, along_x, along_y)
    pieces = []
    split = (((zxy, 1), (xyz, 1), (yxz, 1)), ((xyz, 2), (yxz, 1)), ((xyz, 1), (yxz, 2)))
    for block, row in enumerate(split):
        first = 0
        for order, count in row:
            rows = length = count * units
            stages = []
            for axis, stride, size in order:
                if size == 1:
                    continue
                scatter = length % (size * TILE) == 0
                stages.append((axis, stride, size, length, scatter))
                if scatter:
                    length //= size
            pieces.append((block, first, rows, stages))
            first += rows
    return pieces


def kernel(
    n_grp, n_blk, plan, chunk,
    states_hbm, weight_hbm, attempts_hbm, theorem_hbm, positive_hbm,
    loss, grad_att, res,
    states, weight, attempts, theorem, positive, load_sems,
    weight_t, unit_t, gproj_t, w_all, inv_rms, panel, panel_t,
    ga_stage, ga_core, ga_sum, ga_recv, acc, core_send, core_recv, send_sems, recv_sems, *stage_bufs,
):
    queries, dim = states.shape
    own_att = attempts.shape[0]
    n_att = own_att * n_blk
    half = dim // 2
    width = dim // PARTS
    multiplier = 1.0 / (logit_sharpness * dim)
    grp = lax.axis_index("grp")
    blk = lax.axis_index("blk")
    core = lax.rem(blk, 2)
    sibling = blk + 1 - 2 * core
    used = [0]
    started = []

    def member(axis, stride, size):
        index = grp if axis == "grp" else blk
        return lax.rem(index // stride, size)

    def partner(axis, stride, size, k):
        index = grp if axis == "grp" else blk
        here = lax.rem(index // stride, size)
        there = lax.rem(here + k, size)
        return {axis: index + (there - here) * stride}, there

    def send(src, dst, device):
        n = used[0]
        used[0] += 1
        copy = pltpu.make_async_remote_copy(
            src_ref=src, dst_ref=dst, send_sem=send_sems.at[n], recv_sem=recv_sems.at[n],
            device_id=device, device_id_type=MESH,
        )
        copy.start()
        started.append(copy)
        return copy

    def load(src, dst, n):
        return pltpu.make_async_copy(src, dst, load_sems.at[n])

    def load_states(step):
        rows = pl.ds(pl.multiple_of(step * chunk, chunk), chunk)
        return load(states_hbm.at[rows], states.at[rows], 4 + step)

    loads = [
        load(attempts_hbm, attempts, 0),
        load(weight_hbm, weight, 1),
        load(theorem_hbm, theorem, 2),
        load(positive_hbm, positive, 3),
    ]
    loads[0].start()
    loads[1].start()
    for step in range(queries // chunk):
        load_states(step).start()
    loads[2].start()
    loads[3].start()

    greeted = [("blk", 1, n_blk), ("grp", 1, 2), ("grp", 2, n_grp // 2)]
    barrier = pltpu.get_barrier_semaphore()
    count = 0
    for axis, stride, size in greeted:
        for k in range(1, size):
            pl.semaphore_signal(
                barrier, inc=1, device_id=partner(axis, stride, size, k)[0], device_id_type=MESH
            )
            count += 1

    loads[0].wait()
    att = attempts[...].astype(jnp.float32)
    att_r = lax.rsqrt(jnp.mean(att * att, axis=1, keepdims=True) + epsilon)
    att_unit = att * att_r
    own_rows = pl.ds(pl.multiple_of(blk * own_att, own_att), own_att)
    panel[own_rows, :] = att_unit.astype(jnp.bfloat16)
    pl.semaphore_wait(barrier, count)
    across = [
        send(panel.at[own_rows], panel.at[own_rows], partner("blk", 2, n_blk // 2, k)[0])
        for k in range(1, n_blk // 2)
    ]
    to_sibling = [send(panel.at[own_rows], panel.at[own_rows], {"blk": sibling})]

    loads[1].wait()
    weight_t[...] = weight[...].T

    def project(step, carry):
        load_states(step).wait()
        cols = pl.ds(pl.multiple_of(step * chunk, chunk), chunk)
        proj = lax.dot_general(
            weight_t[...], states[cols, :], NT, preferred_element_type=jnp.float32
        )
        r = lax.rsqrt(jnp.sum(proj * proj, axis=0, keepdims=True) * (1.0 / dim) + epsilon)
        inv_rms[:, cols] = r
        unit_t[:, cols] = (proj * r).astype(jnp.bfloat16)
        return carry

    steps = queries // chunk
    lax.fori_loop(0, steps // 2, project, 0)
    for k, copy in enumerate(across):
        copy.wait_recv()
        source = lax.rem(blk // 2 + n_blk // 2 - (k + 1), n_blk // 2) * 2 + core
        rows = pl.ds(pl.multiple_of(source * own_att, own_att), own_att)
        to_sibling.append(send(panel.at[rows], panel.at[rows], {"blk": sibling}))
    lax.fori_loop(steps // 2, steps, project, 0)

    for copy in to_sibling:
        copy.wait_recv()
    loads[2].wait()
    loads[3].wait()
    panel_t[...] = panel[...].T
    theorem_col = jnp.broadcast_to(theorem[...].astype(jnp.float32), (8, n_att)).T[:, 0:1]

    def contrast(step, carry):
        cols = pl.ds(pl.multiple_of(step * chunk, chunk), chunk)
        unit = unit_t[:, cols]
        scores = jnp.dot(panel[...], unit, preferred_element_type=jnp.float32) * multiplier
        chosen = lax.broadcasted_iota(jnp.int32, scores.shape, 0) == positive[:, cols]
        label = jnp.sum(jnp.where(chosen, theorem_col, 0.0), axis=0, keepdims=True)
        expo = jnp.where(theorem_col == label, jnp.exp(scores), 0.0)
        total = jnp.sum(expo, axis=0, keepdims=True)
        pos_score = jnp.sum(jnp.where(chosen, scores, 0.0), axis=0, keepdims=True)
        loss[:, cols] = jnp.log(total) - pos_score
        w = (expo * (1.0 / total) - jnp.where(chosen, 1.0, 0.0)).astype(jnp.bfloat16)
        w_all[:, cols] = w
        along = jnp.sum(w.astype(jnp.float32) * scores, axis=0, keepdims=True) * (1.0 / dim)
        r = inv_rms[:, cols]
        g = jnp.dot(panel_t[...], w, preferred_element_type=jnp.float32)
        gproj_t[:, cols] = (
            g * (r * multiplier) - unit.astype(jnp.float32) * (r * along)
        ).astype(jnp.bfloat16)
        return carry

    lax.fori_loop(0, steps, contrast, 0)

    begin = [first for block, first, rows, stages in plan]
    pending = [None] * len(plan)
    bufs, n = [], 0
    for block, first, rows, stages in plan:
        bufs.append([(stage_bufs[n + 2 * j], stage_bufs[n + 2 * j + 1]) for j in range(len(stages))])
        n += 2 * len(stages)

    def start_stage(piece, j):
        block = plan[piece][0]
        axis, stride, size, length, scatter = plan[piece][3][j]
        stage, recv = bufs[piece][j]
        here = member(axis, stride, size)
        rows = pl.ds(pl.multiple_of(begin[piece], TILE), length)
        stage[...] = acc[block, core, rows, :].astype(jnp.bfloat16)
        pending[piece] = []
        for k in range(1, size):
            device, there = partner(axis, stride, size, k)
            if scatter:
                part = length // size
                src = stage.at[pl.ds(pl.multiple_of(there * part, TILE), part)]
                pending[piece].append(send(src, recv.at[k - 1], device))
            else:
                pending[piece].append(send(stage, recv.at[here], device))

    def finish_stage(piece, j):
        block = plan[piece][0]
        axis, stride, size, length, scatter = plan[piece][3][j]
        stage, recv = bufs[piece][j]
        here = member(axis, stride, size)
        for copy in pending[piece]:
            copy.wait_recv()
        if scatter:
            part = length // size
            begin[piece] = begin[piece] + here * part
            rows = pl.ds(pl.multiple_of(begin[piece], TILE), part)
            total = acc[block, core, rows, :]
            for k in range(size - 1):
                total = total + recv[k].astype(jnp.float32)
        else:
            rows = pl.ds(pl.multiple_of(begin[piece], TILE), length)
            recv[here] = stage[...]
            total = recv[0].astype(jnp.float32)
            for k in range(1, size):
                total = total + recv[k].astype(jnp.float32)
        if j + 1 < len(plan[piece][3]):
            acc[block, core, rows, :] = total
        else:
            res[core, block, rows, :] = total.astype(jnp.bfloat16)

    def start_back(piece, j):
        block = plan[piece][0]
        axis, stride, size, length, scatter = plan[piece][3][j]
        part = length // size
        rows = pl.ds(pl.multiple_of(begin[piece], TILE), part)
        spot = res.at[core, block, rows]
        pending[piece] = [
            send(spot, spot, partner(axis, stride, size, k)[0]) for k in range(1, size)
        ]
        begin[piece] = begin[piece] - member(axis, stride, size) * part

    def steps_of(piece):
        block, first, rows, stages = plan[piece]
        start_stage(piece, 0)
        yield
        for j in range(len(stages)):
            finish_stage(piece, j)
            if j + 1 < len(stages):
                start_stage(piece, j + 1)
                yield
        for j in reversed(range(len(stages))):
            if stages[j][4]:
                start_back(piece, j)
                yield
                for copy in pending[piece]:
                    copy.wait_recv()
        spot = res.at[core, block, pl.ds(first, rows)]
        pending[piece] = [send(spot, spot, {"blk": sibling})]
        yield
        pending[piece][0].wait_recv()

    runs = [steps_of(piece) for piece in range(len(plan))]

    def advance(block):
        more = False
        for piece in range(len(plan)):
            if plan[piece][0] == block:
                more = next(runs[piece], "end") != "end" or more
        return more

    slabs = half // LANES
    core_copies = []

    def weight_third(block):
        def one_half(which, carry):
            rows = pl.ds(pl.multiple_of(which * half, LANES), half)
            tile = jnp.dot(
                gproj_t[rows, :], states[:, block * width:(block + 1) * width],
                preferred_element_type=jnp.float32,
            ).T
            for e in range(slabs):
                acc[block, which, e * width:(e + 1) * width, :] = tile[:, e * LANES:(e + 1) * LANES]
            return carry

        lax.fori_loop(0, 2, one_half, 0)
        core_send[block] = acc[block, 1 - core].astype(jnp.bfloat16)
        core_copies.append(send(core_send.at[block], core_recv.at[block], {"blk": sibling}))

    def add_sibling(block):
        core_copies[block].wait_recv()
        acc[block, core] += core_recv[block].astype(jnp.float32)

    for block in range(PARTS):
        weight_third(block)
        if block >= 1:
            add_sibling(block - 1)
            advance(block - 1)

    advance(0)
    def att_third(block, carry):
        cols = pl.ds(pl.multiple_of(block * width, LANES), width)
        ga = lax.dot_general(
            unit_t[cols, :], w_all[...], NT, preferred_element_type=jnp.float32
        )
        ga = (ga * multiplier).T.astype(jnp.bfloat16)
        for owner in range(n_blk):
            ga_stage[owner % 2, owner // 2, :, cols] = ga[owner * own_att:(owner + 1) * own_att, :]
        return carry

    lax.fori_loop(0, PARTS, att_third, 0)
    ga_copy = send(ga_stage.at[1 - core], ga_core, {"blk": sibling})
    add_sibling(PARTS - 1)
    advance(PARTS - 1)
    advance(1)
    advance(0)
    advance(2)
    advance(1)
    advance(0)

    ga_copy.wait_recv()
    ga_sum[...] = (
        ga_stage[core].astype(jnp.float32) + ga_core[...].astype(jnp.float32)
    ).astype(jnp.bfloat16)
    ga_copies = []
    for k in range(1, n_blk // 2):
        device, owner = partner("blk", 2, n_blk // 2, k)
        ga_copies.append(send(ga_sum.at[owner], ga_recv.at[k - 1], device))

    advance(2)
    advance(1)
    advance(0)
    advance(2)
    advance(1)
    advance(0)
    for copy in ga_copies:
        copy.wait_recv()
    ga = ga_stage[core, blk // 2].astype(jnp.float32) + ga_core[blk // 2].astype(jnp.float32)
    for k in range(n_blk // 2 - 1):
        ga = ga + ga_recv[k].astype(jnp.float32)
    att = attempts[...].astype(jnp.float32)
    att_r = lax.rsqrt(jnp.mean(att * att, axis=1, keepdims=True) + epsilon)
    att_unit = att * att_r
    grad_att[...] = att_r * (ga - att_unit * jnp.mean(ga * att_unit, axis=1, keepdims=True))

    more = True
    while more:
        more = any([advance(block) for block in (2, 1, 0)])
    for copy in started:
        copy.wait_send()


def write_out(loss, grad_att, res, loss_hbm, grad_att_hbm, grad_w_hbm, wide, sems):
    copies = [
        pltpu.make_async_copy(loss, loss_hbm, sems.at[0]),
        pltpu.make_async_copy(grad_att, grad_att_hbm, sems.at[1]),
    ]
    for copy in copies:
        copy.start()
    dim = wide.shape[0]
    half, width = dim // 2, dim // PARTS
    slabs = half // LANES
    for block in range(PARTS):
        rows = pl.ds(block * width, width)
        for which in range(2):
            for e in range(slabs):
                col = which * half + e * LANES
                wide[rows, col:col + LANES] = (
                    res[which, block, e * width:(e + 1) * width, :].astype(jnp.float32)
                )
        copy = pltpu.make_async_copy(wide.at[rows], grad_w_hbm.at[rows], sems.at[2 + block])
        copy.start()
        copies.append(copy)
    for copy in copies:
        copy.wait()


def on_device(n_grp, n_blk, states, query_weight, attempts, attempt_theorem, positive):
    queries, dim = states.shape
    own_att = attempts.shape[0]
    n_att = own_att * n_blk
    chunk = min(512, queries)
    rows = dim * (dim // 2) // PARTS // LANES
    plan = stage_plan(n_grp, n_blk, rows // 3)
    copies = 2 * n_blk + 2 * PARTS + len(plan)
    bf16, f32 = jnp.bfloat16, jnp.float32
    stage_bufs = []
    for block, first, count, stages in plan:
        for axis, stride, size, length, scatter in stages:
            copies += (size - 1) * (2 if scatter else 1)
            stage_bufs.append(pltpu.VMEM((length, LANES), bf16))
            if scatter:
                stage_bufs.append(pltpu.VMEM((size - 1, length // size, LANES), bf16))
            else:
                stage_bufs.append(pltpu.VMEM((size, length, LANES), bf16))
    vmem = pl.BlockSpec(memory_space=pltpu.VMEM)
    hbm = pl.BlockSpec(memory_space=pltpu.HBM)
    loss, grad_att, res = pl.pallas_call(
        functools.partial(kernel, n_grp, n_blk, plan, chunk),
        out_shape=(
            jax.ShapeDtypeStruct((1, queries), f32),
            jax.ShapeDtypeStruct((own_att, dim), f32),
            jax.ShapeDtypeStruct((2, PARTS, rows, LANES), bf16),
        ),
        in_specs=[hbm] * 5,
        out_specs=(vmem,) * 3,
        scratch_shapes=[
            pltpu.VMEM((queries, dim), bf16),
            pltpu.VMEM((dim, dim), bf16),
            pltpu.VMEM((own_att, dim), bf16),
            pltpu.VMEM((1, n_att), jnp.int32),
            pltpu.VMEM((1, queries), jnp.int32),
            pltpu.SemaphoreType.DMA((4 + queries // chunk,)),
            pltpu.VMEM((dim, dim), bf16),
            pltpu.VMEM((dim, queries), bf16),
            pltpu.VMEM((dim, queries), bf16),
            pltpu.VMEM((n_att, queries), bf16),
            pltpu.VMEM((1, queries), f32),
            pltpu.VMEM((n_att, dim), bf16),
            pltpu.VMEM((dim, n_att), bf16),
            pltpu.VMEM((2, n_blk // 2, own_att, dim), bf16),
            pltpu.VMEM((n_blk // 2, own_att, dim), bf16),
            pltpu.VMEM((n_blk // 2, own_att, dim), bf16),
            pltpu.VMEM((max(n_blk // 2 - 1, 1), own_att, dim), bf16),
            pltpu.VMEM((PARTS, 2, rows, LANES), f32),
            pltpu.VMEM((PARTS, rows, LANES), bf16),
            pltpu.VMEM((PARTS, rows, LANES), bf16),
            pltpu.SemaphoreType.DMA((copies,)),
            pltpu.SemaphoreType.DMA((copies,)),
            *stage_bufs,
        ],
        compiler_params=pltpu.CompilerParams(
            collective_id=0, has_side_effects=True, vmem_limit_bytes=48 * 1024 * 1024
        ),
    )(*[pltpu.with_memory_space_constraint(x, pltpu.HBM) for x in (states, query_weight, attempts, attempt_theorem.reshape(1, n_att), positive.reshape(1, queries))])
    loss, grad_att, grad_w = pl.pallas_call(
        write_out,
        out_shape=(
            jax.ShapeDtypeStruct((1, queries), f32),
            jax.ShapeDtypeStruct((own_att, dim), f32),
            jax.ShapeDtypeStruct((dim, dim), f32),
        ),
        in_specs=[vmem] * 3,
        out_specs=(hbm,) * 3,
        scratch_shapes=[pltpu.VMEM((dim, dim), f32), pltpu.SemaphoreType.DMA((2 + PARTS,))],
        compiler_params=pltpu.CompilerParams(vmem_limit_bytes=8 * 1024 * 1024),
    )(loss, grad_att, res)
    return loss.reshape(queries), grad_att, grad_w


def solution(mesh):
    n_grp, n_blk = mesh.shape["grp"], mesh.shape["blk"]
    in_specs = (P(("grp", "blk"), None), P(), P(("grp", "blk"), None), P("grp"), P(("grp", "blk")))
    out_specs = (P(("grp", "blk")), P(("grp", "blk"), None), P())
    return jax.shard_map(
        functools.partial(on_device, n_grp, n_blk),
        mesh=mesh, in_specs=in_specs, out_specs=out_specs, check_vma=False,
    )
```

```python
import functools

import jax
import jax.numpy as jnp
from jax import lax
from jax.experimental import pallas as pl
from jax.experimental.pallas import tpu as pltpu
from jax.sharding import PartitionSpec as P

logit_sharpness = 0.07
epsilon = 1e-06
MESH = pl.DeviceIdType.MESH
PARTS = 3
LANES = 128
TILE = 16
NT = (((1,), (1,)), ((), ()))


def stage_plan(n_grp, n_blk, units):
    along_x = ("blk", 2, n_blk // 2)
    along_y = ("grp", 1, 2)
    along_z = ("grp", 2, n_grp // 2)
    xyz, yxz = (along_x, along_y, along_z), (along_y, along_x, along_z)
    pieces = []
    split = (((xyz, 3),), ((yxz, 3),), ((xyz, 2), (yxz, 1)))
    for block, row in enumerate(split):
        first = 0
        for order, count in row:
            rows = length = count * units
            stages = []
            for axis, stride, size in order:
                if size == 1:
                    continue
                scatter = length % (size * TILE) == 0
                stages.append((axis, stride, size, length, scatter))
                if scatter:
                    length //= size
            pieces.append((block, first, rows, stages))
            first += rows
    return pieces


def kernel(
    n_grp, n_blk, plan, chunk,
    states_hbm, weight_hbm, attempts_hbm, theorem_hbm, positive_hbm,
    loss, grad_att, res,
    states, weight, attempts, theorem, positive, load_sems,
    weight_t, unit_t, gproj_t, w_all, inv_rms, along_all, panel, panel_t,
    ga_stage, ga_core, ga_sum, ga_recv, acc, core_send, core_recv, send_sems, recv_sems, *stage_bufs,
):
    queries, dim = states.shape
    own_att = attempts.shape[0]
    n_att = own_att * n_blk
    half = dim // 2
    width = dim // PARTS
    multiplier = 1.0 / (logit_sharpness * dim)
    grp = lax.axis_index("grp")
    blk = lax.axis_index("blk")
    core = lax.rem(blk, 2)
    sibling = blk + 1 - 2 * core
    used = [0]

    def member(axis, stride, size):
        index = grp if axis == "grp" else blk
        return lax.rem(index // stride, size)

    def partner(axis, stride, size, k):
        index = grp if axis == "grp" else blk
        here = lax.rem(index // stride, size)
        there = lax.rem(here + k, size)
        return {axis: index + (there - here) * stride}, there

    def send(src, dst, device):
        n = used[0]
        used[0] += 1
        copy = pltpu.make_async_remote_copy(
            src_ref=src, dst_ref=dst, send_sem=send_sems.at[n], recv_sem=recv_sems.at[n],
            device_id=device, device_id_type=MESH,
        )
        copy.start()
        return copy

    def load(src, dst, n):
        return pltpu.make_async_copy(src, dst, load_sems.at[n])

    def load_states(step):
        rows = pl.ds(pl.multiple_of(step * chunk, chunk), chunk)
        return load(states_hbm.at[rows], states.at[rows], 4 + step)

    loads = [
        load(attempts_hbm, attempts, 0),
        load(weight_hbm, weight, 1),
        load(theorem_hbm, theorem, 2),
        load(positive_hbm, positive, 3),
    ]
    loads[0].start()
    loads[1].start()
    for step in range(queries // chunk):
        load_states(step).start()
    loads[2].start()
    loads[3].start()

    greeted = [("blk", 1, n_blk), ("grp", 1, 2), ("grp", 2, n_grp // 2)]
    barrier = pltpu.get_barrier_semaphore()
    count = 0
    for axis, stride, size in greeted:
        for k in range(1, size):
            pl.semaphore_signal(
                barrier, inc=1, device_id=partner(axis, stride, size, k)[0], device_id_type=MESH
            )
            count += 1

    loads[0].wait()
    att = attempts[...].astype(jnp.float32)
    att_r = lax.rsqrt(jnp.mean(att * att, axis=1, keepdims=True) + epsilon)
    att_unit = att * att_r
    own_rows = pl.ds(pl.multiple_of(blk * own_att, own_att), own_att)
    panel[own_rows, :] = att_unit.astype(jnp.bfloat16)
    pl.semaphore_wait(barrier, count)
    across = [
        send(panel.at[own_rows], panel.at[own_rows], partner("blk", 2, n_blk // 2, k)[0])
        for k in range(1, n_blk // 2)
    ]
    to_sibling = [send(panel.at[own_rows], panel.at[own_rows], {"blk": sibling})]

    loads[1].wait()
    weight_t[...] = weight[...].T

    def project(step, carry):
        load_states(step).wait()
        cols = pl.ds(pl.multiple_of(step * chunk, chunk), chunk)
        proj = lax.dot_general(
            weight_t[...], states[cols, :], NT, preferred_element_type=jnp.float32
        )
        r = lax.rsqrt(jnp.sum(proj * proj, axis=0, keepdims=True) * (1.0 / dim) + epsilon)
        inv_rms[:, cols] = r
        unit_t[:, cols] = (proj * r).astype(jnp.bfloat16)
        return carry

    steps = queries // chunk
    lax.fori_loop(0, steps // 2, project, 0)
    for k, copy in enumerate(across):
        copy.wait()
        source = lax.rem(blk // 2 + n_blk // 2 - (k + 1), n_blk // 2) * 2 + core
        rows = pl.ds(pl.multiple_of(source * own_att, own_att), own_att)
        to_sibling.append(send(panel.at[rows], panel.at[rows], {"blk": sibling}))
    lax.fori_loop(steps // 2, steps, project, 0)

    for copy in to_sibling:
        copy.wait()
    loads[2].wait()
    loads[3].wait()
    panel_t[...] = panel[...].T
    theorem_col = jnp.broadcast_to(theorem[...].astype(jnp.float32), (8, n_att)).T[:, 0:1]

    def contrast(step, carry):
        cols = pl.ds(pl.multiple_of(step * chunk, chunk), chunk)
        unit = unit_t[:, cols]
        scores = jnp.dot(panel[...], unit, preferred_element_type=jnp.float32) * multiplier
        chosen = lax.broadcasted_iota(jnp.int32, scores.shape, 0) == positive[:, cols]
        label = jnp.sum(jnp.where(chosen, theorem_col, 0.0), axis=0, keepdims=True)
        expo = jnp.where(theorem_col == label, jnp.exp(scores), 0.0)
        total = jnp.sum(expo, axis=0, keepdims=True)
        pos_score = jnp.sum(jnp.where(chosen, scores, 0.0), axis=0, keepdims=True)
        loss[:, cols] = jnp.log(total) - pos_score
        w = (expo * (1.0 / total) - jnp.where(chosen, 1.0, 0.0)).astype(jnp.bfloat16)
        w_all[:, cols] = w
        along = jnp.sum(w.astype(jnp.float32) * scores, axis=0, keepdims=True) * (1.0 / dim)
        along_all[:, cols] = along * inv_rms[:, cols]
        return carry

    lax.fori_loop(0, steps, contrast, 0)

    begin = [first for block, first, rows, stages in plan]
    pending = [None] * len(plan)
    bufs, n = [], 0
    for block, first, rows, stages in plan:
        bufs.append([(stage_bufs[n + 2 * j], stage_bufs[n + 2 * j + 1]) for j in range(len(stages))])
        n += 2 * len(stages)

    def start_stage(piece, j):
        block = plan[piece][0]
        axis, stride, size, length, scatter = plan[piece][3][j]
        stage, recv = bufs[piece][j]
        here = member(axis, stride, size)
        rows = pl.ds(pl.multiple_of(begin[piece], TILE), length)
        stage[...] = acc[block, rows, :].astype(jnp.bfloat16)
        pending[piece] = []
        for k in range(1, size):
            device, there = partner(axis, stride, size, k)
            if scatter:
                part = length // size
                src = stage.at[pl.ds(pl.multiple_of(there * part, TILE), part)]
                pending[piece].append(send(src, recv.at[k - 1], device))
            else:
                pending[piece].append(send(stage, recv.at[here], device))

    def finish_stage(piece, j):
        block = plan[piece][0]
        axis, stride, size, length, scatter = plan[piece][3][j]
        stage, recv = bufs[piece][j]
        here = member(axis, stride, size)
        for copy in pending[piece]:
            copy.wait()
        if scatter:
            part = length // size
            begin[piece] = begin[piece] + here * part
            rows = pl.ds(pl.multiple_of(begin[piece], TILE), part)
            total = acc[block, rows, :]
            for k in range(size - 1):
                total = total + recv[k].astype(jnp.float32)
        else:
            rows = pl.ds(pl.multiple_of(begin[piece], TILE), length)
            recv[here] = stage[...]
            total = recv[0].astype(jnp.float32)
            for k in range(1, size):
                total = total + recv[k].astype(jnp.float32)
        if j + 1 < len(plan[piece][3]):
            acc[block, rows, :] = total
        else:
            res[core, block, rows, :] = total.astype(jnp.bfloat16)

    def start_back(piece, j):
        block = plan[piece][0]
        axis, stride, size, length, scatter = plan[piece][3][j]
        part = length // size
        rows = pl.ds(pl.multiple_of(begin[piece], TILE), part)
        spot = res.at[core, block, rows]
        pending[piece] = [
            send(spot, spot, partner(axis, stride, size, k)[0]) for k in range(1, size)
        ]
        begin[piece] = begin[piece] - member(axis, stride, size) * part

    def steps_of(piece):
        block, first, rows, stages = plan[piece]
        start_stage(piece, 0)
        yield
        for j in range(len(stages)):
            finish_stage(piece, j)
            if j + 1 < len(stages):
                start_stage(piece, j + 1)
                yield
        for j in reversed(range(len(stages))):
            if stages[j][4]:
                start_back(piece, j)
                yield
                for copy in pending[piece]:
                    copy.wait()
        spot = res.at[core, block, pl.ds(first, rows)]
        pending[piece] = [send(spot, spot, {"blk": sibling})]
        yield
        pending[piece][0].wait()

    runs = [steps_of(piece) for piece in range(len(plan))]

    def advance(block):
        more = False
        for piece in range(len(plan)):
            if plan[piece][0] == block:
                more = next(runs[piece], "end") != "end" or more
        return more

    slabs = width // LANES
    subs = half // LANES
    core_copies = []

    def grad_proj_third(block):
        rows = slice(block * width, (block + 1) * width)
        g = jnp.dot(panel_t[rows, :], w_all[...], preferred_element_type=jnp.float32)
        gproj_t[rows, :] = (
            g * (inv_rms[...] * multiplier) - unit_t[rows, :].astype(jnp.float32) * along_all[...]
        ).astype(jnp.bfloat16)

    def weight_third(block):
        rows = slice(block * width, (block + 1) * width)
        for which, keep in ((1 - core, False), (core, True)):
            cols = pl.ds(pl.multiple_of(which * half, half), half)
            tile = jnp.dot(
                gproj_t[rows, :], states[:, cols], preferred_element_type=jnp.float32
            ).T
            for u in range(subs):
                for e in range(slabs):
                    at = slice((u * slabs + e) * LANES, (u * slabs + e + 1) * LANES)
                    value = tile[u * LANES:(u + 1) * LANES, e * LANES:(e + 1) * LANES]
                    if keep:
                        acc[block, at, :] = value
                    else:
                        core_send[block, at, :] = value.astype(jnp.bfloat16)
            if not keep:
                core_copies.append(send(core_send.at[block], core_recv.at[block], {"blk": sibling}))

    def add_sibling(block):
        core_copies[block].wait()
        acc[block] += core_recv[block].astype(jnp.float32)

    for block in range(PARTS):
        grad_proj_third(block)
        if block >= 1:
            add_sibling(block - 1)
            advance(block - 1)
        weight_third(block)

    advance(0)
    ga = lax.dot_general(unit_t[...], w_all[...], NT, preferred_element_type=jnp.float32)
    ga = (ga * multiplier).T.astype(jnp.bfloat16)
    for owner in range(n_blk):
        ga_stage[owner % 2, owner // 2] = ga[owner * own_att:(owner + 1) * own_att, :]
    ga_copy = send(ga_stage.at[1 - core], ga_core, {"blk": sibling})
    add_sibling(PARTS - 1)
    advance(PARTS - 1)
    advance(1)
    advance(0)
    advance(2)
    advance(1)
    advance(0)

    ga_copy.wait()
    ga_sum[...] = (
        ga_stage[core].astype(jnp.float32) + ga_core[...].astype(jnp.float32)
    ).astype(jnp.bfloat16)
    ga_copies = []
    for k in range(1, n_blk // 2):
        device, owner = partner("blk", 2, n_blk // 2, k)
        ga_copies.append(send(ga_sum.at[owner], ga_recv.at[k - 1], device))

    advance(2)
    advance(1)
    advance(0)
    advance(2)
    advance(1)
    advance(0)
    for copy in ga_copies:
        copy.wait()
    ga = ga_stage[core, blk // 2].astype(jnp.float32) + ga_core[blk // 2].astype(jnp.float32)
    for k in range(n_blk // 2 - 1):
        ga = ga + ga_recv[k].astype(jnp.float32)
    att = attempts[...].astype(jnp.float32)
    att_r = lax.rsqrt(jnp.mean(att * att, axis=1, keepdims=True) + epsilon)
    att_unit = att * att_r
    grad_att[...] = att_r * (ga - att_unit * jnp.mean(ga * att_unit, axis=1, keepdims=True))

    more = True
    while more:
        more = any([advance(block) for block in (2, 1, 0)])


def write_out(loss, grad_att, res, loss_hbm, grad_att_hbm, grad_w_hbm, wide, sems):
    copies = [
        pltpu.make_async_copy(loss, loss_hbm, sems.at[0]),
        pltpu.make_async_copy(grad_att, grad_att_hbm, sems.at[1]),
    ]
    for copy in copies:
        copy.start()
    dim = wide.shape[0]
    half, width = dim // 2, dim // PARTS
    slabs, subs = width // LANES, half // LANES
    for which in range(2):
        for u in range(subs):
            row = which * half + u * LANES
            for block in range(PARTS):
                for e in range(slabs):
                    at = (u * slabs + e) * LANES
                    col = block * width + e * LANES
                    wide[row:row + LANES, col:col + LANES] = (
                        res[which, block, at:at + LANES, :].astype(jnp.float32)
                    )
            rows = pl.ds(row, LANES)
            copy = pltpu.make_async_copy(
                wide.at[rows], grad_w_hbm.at[rows], sems.at[2 + which * subs + u]
            )
            copy.start()
            copies.append(copy)
    for copy in copies:
        copy.wait()


def on_device(n_grp, n_blk, states, query_weight, attempts, attempt_theorem, positive):
    queries, dim = states.shape
    own_att = attempts.shape[0]
    n_att = own_att * n_blk
    chunk = min(512, queries)
    rows = dim * (dim // 2) // PARTS // LANES
    plan = stage_plan(n_grp, n_blk, rows // 3)
    copies = 2 * n_blk + 2 * PARTS + len(plan)
    bf16, f32 = jnp.bfloat16, jnp.float32
    stage_bufs = []
    for block, first, count, stages in plan:
        for axis, stride, size, length, scatter in stages:
            copies += (size - 1) * (2 if scatter else 1)
            stage_bufs.append(pltpu.VMEM((length, LANES), bf16))
            if scatter:
                stage_bufs.append(pltpu.VMEM((size - 1, length // size, LANES), bf16))
            else:
                stage_bufs.append(pltpu.VMEM((size, length, LANES), bf16))
    vmem = pl.BlockSpec(memory_space=pltpu.VMEM)
    hbm = pl.BlockSpec(memory_space=pltpu.HBM)
    loss, grad_att, res = pl.pallas_call(
        functools.partial(kernel, n_grp, n_blk, plan, chunk),
        out_shape=(
            jax.ShapeDtypeStruct((1, queries), f32),
            jax.ShapeDtypeStruct((own_att, dim), f32),
            jax.ShapeDtypeStruct((2, PARTS, rows, LANES), bf16),
        ),
        in_specs=[hbm] * 5,
        out_specs=(vmem,) * 3,
        scratch_shapes=[
            pltpu.VMEM((queries, dim), bf16),
            pltpu.VMEM((dim, dim), bf16),
            pltpu.VMEM((own_att, dim), bf16),
            pltpu.VMEM((1, n_att), jnp.int32),
            pltpu.VMEM((1, queries), jnp.int32),
            pltpu.SemaphoreType.DMA((4 + queries // chunk,)),
            pltpu.VMEM((dim, dim), bf16),
            pltpu.VMEM((dim, queries), bf16),
            pltpu.VMEM((dim, queries), bf16),
            pltpu.VMEM((n_att, queries), bf16),
            pltpu.VMEM((1, queries), f32),
            pltpu.VMEM((1, queries), f32),
            pltpu.VMEM((n_att, dim), bf16),
            pltpu.VMEM((dim, n_att), bf16),
            pltpu.VMEM((2, n_blk // 2, own_att, dim), bf16),
            pltpu.VMEM((n_blk // 2, own_att, dim), bf16),
            pltpu.VMEM((n_blk // 2, own_att, dim), bf16),
            pltpu.VMEM((max(n_blk // 2 - 1, 1), own_att, dim), bf16),
            pltpu.VMEM((PARTS, rows, LANES), f32),
            pltpu.VMEM((PARTS, rows, LANES), bf16),
            pltpu.VMEM((PARTS, rows, LANES), bf16),
            pltpu.SemaphoreType.DMA((copies,)),
            pltpu.SemaphoreType.DMA((copies,)),
            *stage_bufs,
        ],
        compiler_params=pltpu.CompilerParams(
            collective_id=0, has_side_effects=True, vmem_limit_bytes=48 * 1024 * 1024
        ),
    )(*[pltpu.with_memory_space_constraint(x, pltpu.HBM) for x in (states, query_weight, attempts, attempt_theorem.reshape(1, n_att), positive.reshape(1, queries))])
    loss, grad_att, grad_w = pl.pallas_call(
        write_out,
        out_shape=(
            jax.ShapeDtypeStruct((1, queries), f32),
            jax.ShapeDtypeStruct((own_att, dim), f32),
            jax.ShapeDtypeStruct((dim, dim), f32),
        ),
        in_specs=[vmem] * 3,
        out_specs=(hbm,) * 3,
        scratch_shapes=[pltpu.VMEM((dim, dim), f32), pltpu.SemaphoreType.DMA((2 + dim // LANES,))],
        compiler_params=pltpu.CompilerParams(vmem_limit_bytes=8 * 1024 * 1024),
    )(loss, grad_att, res)
    return loss.reshape(queries), grad_att, grad_w


def solution(mesh):
    n_grp, n_blk = mesh.shape["grp"], mesh.shape["blk"]
    in_specs = (P(("grp", "blk"), None), P(), P(("grp", "blk"), None), P("grp"), P(("grp", "blk")))
    out_specs = (P(("grp", "blk")), P(("grp", "blk"), None), P())
    return jax.shard_map(
        functools.partial(on_device, n_grp, n_blk),
        mesh=mesh, in_specs=in_specs, out_specs=out_specs, check_vma=False,
    )
```

```python
import functools

import jax
import jax.numpy as jnp
from jax import lax
from jax.experimental import pallas as pl
from jax.experimental.pallas import tpu as pltpu
from jax.sharding import PartitionSpec as P

logit_sharpness = 0.07
epsilon = 1e-06
MESH = pl.DeviceIdType.MESH
PARTS = 3
LANES = 128
TILE = 16
NT = (((1,), (1,)), ((), ()))


def stage_plan(n_grp, n_blk, units):
    along_x = ("blk", 2, n_blk // 2)
    along_y = ("grp", 1, 2)
    along_z = ("grp", 2, n_grp // 2)
    xyz, yxz = (along_x, along_y, along_z), (along_y, along_x, along_z)
    pieces = []
    split = (((xyz, 3),), ((yxz, 3),), ((xyz, 2), (yxz, 1)))
    for block, row in enumerate(split):
        first = 0
        for order, count in row:
            rows = length = count * units
            stages = []
            for axis, stride, size in order:
                if size == 1:
                    continue
                scatter = length % (size * TILE) == 0
                stages.append((axis, stride, size, length, scatter))
                if scatter:
                    length //= size
            pieces.append((block, first, rows, stages))
            first += rows
    return pieces


def kernel(
    n_grp, n_blk, plan, chunk,
    states_hbm, weight_hbm, attempts_hbm, theorem_hbm, positive_hbm,
    loss, grad_att, res,
    states, weight, attempts, theorem, positive, load_sems,
    weight_t, proj_t, gproj_t, w_all, w_scaled, inv_rms, along_all, panel, panel_t,
    ga_stage, ga_core, ga_sum, ga_recv, acc, core_send, core_recv, send_sems, recv_sems, *stage_bufs,
):
    queries, dim = states.shape
    own_att = attempts.shape[0]
    n_att = own_att * n_blk
    half = dim // 2
    width = dim // PARTS
    multiplier = 1.0 / (logit_sharpness * dim)
    grp = lax.axis_index("grp")
    blk = lax.axis_index("blk")
    core = lax.rem(blk, 2)
    sibling = blk + 1 - 2 * core
    used = [0]

    def member(axis, stride, size):
        index = grp if axis == "grp" else blk
        return lax.rem(index // stride, size)

    def partner(axis, stride, size, k):
        index = grp if axis == "grp" else blk
        here = lax.rem(index // stride, size)
        there = lax.rem(here + k, size)
        return {axis: index + (there - here) * stride}, there

    def send(src, dst, device):
        n = used[0]
        used[0] += 1
        copy = pltpu.make_async_remote_copy(
            src_ref=src, dst_ref=dst, send_sem=send_sems.at[n], recv_sem=recv_sems.at[n],
            device_id=device, device_id_type=MESH,
        )
        copy.start()
        return copy

    def load(src, dst, n):
        return pltpu.make_async_copy(src, dst, load_sems.at[n])

    def load_states(step):
        rows = pl.ds(pl.multiple_of(step * chunk, chunk), chunk)
        return load(states_hbm.at[rows], states.at[rows], 4 + step)

    loads = [
        load(attempts_hbm, attempts, 0),
        load(weight_hbm, weight, 1),
        load(theorem_hbm, theorem, 2),
        load(positive_hbm, positive, 3),
    ]
    loads[0].start()
    loads[1].start()
    for step in range(queries // chunk):
        load_states(step).start()
    loads[2].start()
    loads[3].start()

    greeted = [("blk", 1, n_blk), ("grp", 1, 2), ("grp", 2, n_grp // 2)]
    barrier = pltpu.get_barrier_semaphore()
    count = 0
    for axis, stride, size in greeted:
        for k in range(1, size):
            pl.semaphore_signal(
                barrier, inc=1, device_id=partner(axis, stride, size, k)[0], device_id_type=MESH
            )
            count += 1

    loads[0].wait()
    att = attempts[...].astype(jnp.float32)
    att_r = lax.rsqrt(jnp.mean(att * att, axis=1, keepdims=True) + epsilon)
    att_unit = att * att_r
    own_rows = pl.ds(pl.multiple_of(blk * own_att, own_att), own_att)
    panel[own_rows, :] = att_unit.astype(jnp.bfloat16)
    pl.semaphore_wait(barrier, count)
    across = [
        send(panel.at[own_rows], panel.at[own_rows], partner("blk", 2, n_blk // 2, k)[0])
        for k in range(1, n_blk // 2)
    ]
    to_sibling = [send(panel.at[own_rows], panel.at[own_rows], {"blk": sibling})]

    loads[1].wait()
    weight_t[...] = weight[...].T

    def project(step, carry):
        load_states(step).wait()
        cols = pl.ds(pl.multiple_of(step * chunk, chunk), chunk)
        proj = lax.dot_general(
            weight_t[...], states[cols, :], NT, preferred_element_type=jnp.float32
        )
        r = lax.rsqrt(jnp.sum(proj * proj, axis=0, keepdims=True) * (1.0 / dim) + epsilon)
        inv_rms[:, cols] = r
        proj_t[:, cols] = proj.astype(jnp.bfloat16)
        return carry

    steps = queries // chunk
    lax.fori_loop(0, steps // 2, project, 0)
    for k, copy in enumerate(across):
        copy.wait()
        source = lax.rem(blk // 2 + n_blk // 2 - (k + 1), n_blk // 2) * 2 + core
        rows = pl.ds(pl.multiple_of(source * own_att, own_att), own_att)
        to_sibling.append(send(panel.at[rows], panel.at[rows], {"blk": sibling}))
    lax.fori_loop(steps // 2, steps, project, 0)

    for copy in to_sibling:
        copy.wait()
    loads[2].wait()
    loads[3].wait()
    panel_t[...] = panel[...].T
    theorem_col = jnp.broadcast_to(theorem[...].astype(jnp.float32), (8, n_att)).T[:, 0:1]

    def contrast(step, carry):
        cols = pl.ds(pl.multiple_of(step * chunk, chunk), chunk)
        r = inv_rms[:, cols]
        scores = jnp.dot(panel[...], proj_t[:, cols], preferred_element_type=jnp.float32)
        scores = scores * (r * multiplier)
        chosen = lax.broadcasted_iota(jnp.int32, scores.shape, 0) == positive[:, cols]
        label = jnp.sum(jnp.where(chosen, theorem_col, 0.0), axis=0, keepdims=True)
        expo = jnp.where(theorem_col == label, jnp.exp(scores), 0.0)
        total = jnp.sum(expo, axis=0, keepdims=True)
        pos_score = jnp.sum(jnp.where(chosen, scores, 0.0), axis=0, keepdims=True)
        loss[:, cols] = jnp.log(total) - pos_score
        w = (expo * (1.0 / total) - jnp.where(chosen, 1.0, 0.0)).astype(jnp.bfloat16)
        w_all[:, cols] = w
        w_scaled[:, cols] = (w.astype(jnp.float32) * r).astype(jnp.bfloat16)
        along = jnp.sum(w.astype(jnp.float32) * scores, axis=0, keepdims=True) * (1.0 / dim)
        along_all[:, cols] = along * r * r
        return carry

    lax.fori_loop(0, steps, contrast, 0)

    begin = [first for block, first, rows, stages in plan]
    pending = [None] * len(plan)
    bufs, n = [], 0
    for block, first, rows, stages in plan:
        bufs.append([(stage_bufs[n + 2 * j], stage_bufs[n + 2 * j + 1]) for j in range(len(stages))])
        n += 2 * len(stages)

    def start_stage(piece, j):
        block = plan[piece][0]
        axis, stride, size, length, scatter = plan[piece][3][j]
        stage, recv = bufs[piece][j]
        here = member(axis, stride, size)
        rows = pl.ds(pl.multiple_of(begin[piece], TILE), length)
        stage[...] = acc[block, rows, :].astype(jnp.bfloat16)
        pending[piece] = []
        for k in range(1, size):
            device, there = partner(axis, stride, size, k)
            if scatter:
                part = length // size
                src = stage.at[pl.ds(pl.multiple_of(there * part, TILE), part)]
                pending[piece].append(send(src, recv.at[k - 1], device))
            else:
                pending[piece].append(send(stage, recv.at[here], device))

    def finish_stage(piece, j):
        block = plan[piece][0]
        axis, stride, size, length, scatter = plan[piece][3][j]
        stage, recv = bufs[piece][j]
        here = member(axis, stride, size)
        for copy in pending[piece]:
            copy.wait()
        if scatter:
            part = length // size
            begin[piece] = begin[piece] + here * part
            rows = pl.ds(pl.multiple_of(begin[piece], TILE), part)
            total = acc[block, rows, :]
            for k in range(size - 1):
                total = total + recv[k].astype(jnp.float32)
        else:
            rows = pl.ds(pl.multiple_of(begin[piece], TILE), length)
            recv[here] = stage[...]
            total = recv[0].astype(jnp.float32)
            for k in range(1, size):
                total = total + recv[k].astype(jnp.float32)
        if j + 1 < len(plan[piece][3]):
            acc[block, rows, :] = total
        else:
            res[core, block, rows, :] = total.astype(jnp.bfloat16)

    def start_back(piece, j):
        block = plan[piece][0]
        axis, stride, size, length, scatter = plan[piece][3][j]
        part = length // size
        rows = pl.ds(pl.multiple_of(begin[piece], TILE), part)
        spot = res.at[core, block, rows]
        pending[piece] = [
            send(spot, spot, partner(axis, stride, size, k)[0]) for k in range(1, size)
        ]
        begin[piece] = begin[piece] - member(axis, stride, size) * part

    def steps_of(piece):
        block, first, rows, stages = plan[piece]
        start_stage(piece, 0)
        yield
        for j in range(len(stages)):
            finish_stage(piece, j)
            if j + 1 < len(stages):
                start_stage(piece, j + 1)
                yield
        for j in reversed(range(len(stages))):
            if stages[j][4]:
                start_back(piece, j)
                yield
                for copy in pending[piece]:
                    copy.wait()
        spot = res.at[core, block, pl.ds(first, rows)]
        pending[piece] = [send(spot, spot, {"blk": sibling})]
        yield
        pending[piece][0].wait()

    runs = [steps_of(piece) for piece in range(len(plan))]

    def advance(block):
        more = False
        for piece in range(len(plan)):
            if plan[piece][0] == block:
                more = next(runs[piece], "end") != "end" or more
        return more

    slabs = width // LANES
    subs = half // LANES
    core_copies = []

    def grad_proj_third(block):
        rows = slice(block * width, (block + 1) * width)
        g = jnp.dot(panel_t[rows, :], w_all[...], preferred_element_type=jnp.float32)
        gproj_t[rows, :] = (
            g * (inv_rms[...] * multiplier) - proj_t[rows, :].astype(jnp.float32) * along_all[...]
        ).astype(jnp.bfloat16)

    def weight_third(block):
        rows = slice(block * width, (block + 1) * width)
        for which, keep in ((1 - core, False), (core, True)):
            cols = pl.ds(pl.multiple_of(which * half, half), half)
            tile = jnp.dot(
                gproj_t[rows, :], states[:, cols], preferred_element_type=jnp.float32
            ).T
            for u in range(subs):
                for e in range(slabs):
                    at = slice((u * slabs + e) * LANES, (u * slabs + e + 1) * LANES)
                    value = tile[u * LANES:(u + 1) * LANES, e * LANES:(e + 1) * LANES]
                    if keep:
                        acc[block, at, :] = value
                    else:
                        core_send[block, at, :] = value.astype(jnp.bfloat16)
            if not keep:
                core_copies.append(send(core_send.at[block], core_recv.at[block], {"blk": sibling}))

    def add_sibling(block):
        core_copies[block].wait()
        acc[block] += core_recv[block].astype(jnp.float32)

    for block in range(PARTS):
        grad_proj_third(block)
        if block >= 1:
            add_sibling(block - 1)
            advance(block - 1)
        weight_third(block)

    advance(0)
    ga = lax.dot_general(proj_t[...], w_scaled[...], NT, preferred_element_type=jnp.float32)
    ga = (ga * multiplier).T.astype(jnp.bfloat16)
    for owner in range(n_blk):
        ga_stage[owner % 2, owner // 2] = ga[owner * own_att:(owner + 1) * own_att, :]
    ga_copy = send(ga_stage.at[1 - core], ga_core, {"blk": sibling})
    add_sibling(PARTS - 1)
    advance(PARTS - 1)
    advance(1)
    advance(0)
    advance(2)
    advance(1)
    advance(0)

    ga_copy.wait()
    ga_sum[...] = (
        ga_stage[core].astype(jnp.float32) + ga_core[...].astype(jnp.float32)
    ).astype(jnp.bfloat16)
    ga_copies = []
    for k in range(1, n_blk // 2):
        device, owner = partner("blk", 2, n_blk // 2, k)
        ga_copies.append(send(ga_sum.at[owner], ga_recv.at[k - 1], device))

    advance(2)
    advance(1)
    advance(0)
    advance(2)
    advance(1)
    advance(0)
    for copy in ga_copies:
        copy.wait()
    ga = ga_stage[core, blk // 2].astype(jnp.float32) + ga_core[blk // 2].astype(jnp.float32)
    for k in range(n_blk // 2 - 1):
        ga = ga + ga_recv[k].astype(jnp.float32)
    att = attempts[...].astype(jnp.float32)
    att_r = lax.rsqrt(jnp.mean(att * att, axis=1, keepdims=True) + epsilon)
    att_unit = att * att_r
    grad_att[...] = att_r * (ga - att_unit * jnp.mean(ga * att_unit, axis=1, keepdims=True))

    more = True
    while more:
        more = any([advance(block) for block in (2, 1, 0)])


def write_out(loss, grad_att, res, loss_hbm, grad_att_hbm, grad_w_hbm, wide, sems):
    copies = [
        pltpu.make_async_copy(loss, loss_hbm, sems.at[0]),
        pltpu.make_async_copy(grad_att, grad_att_hbm, sems.at[1]),
    ]
    for copy in copies:
        copy.start()
    dim = wide.shape[0]
    half, width = dim // 2, dim // PARTS
    slabs, subs = width // LANES, half // LANES
    for which in range(2):
        for u in range(subs):
            row = which * half + u * LANES
            for block in range(PARTS):
                for e in range(slabs):
                    at = (u * slabs + e) * LANES
                    col = block * width + e * LANES
                    wide[row:row + LANES, col:col + LANES] = (
                        res[which, block, at:at + LANES, :].astype(jnp.float32)
                    )
            rows = pl.ds(row, LANES)
            copy = pltpu.make_async_copy(
                wide.at[rows], grad_w_hbm.at[rows], sems.at[2 + which * subs + u]
            )
            copy.start()
            copies.append(copy)
    for copy in copies:
        copy.wait()


def on_device(n_grp, n_blk, states, query_weight, attempts, attempt_theorem, positive):
    queries, dim = states.shape
    own_att = attempts.shape[0]
    n_att = own_att * n_blk
    chunk = min(512, queries)
    rows = dim * (dim // 2) // PARTS // LANES
    plan = stage_plan(n_grp, n_blk, rows // 3)
    copies = 2 * n_blk + 2 * PARTS + len(plan)
    bf16, f32 = jnp.bfloat16, jnp.float32
    stage_bufs = []
    for block, first, count, stages in plan:
        for axis, stride, size, length, scatter in stages:
            copies += (size - 1) * (2 if scatter else 1)
            stage_bufs.append(pltpu.VMEM((length, LANES), bf16))
            if scatter:
                stage_bufs.append(pltpu.VMEM((size - 1, length // size, LANES), bf16))
            else:
                stage_bufs.append(pltpu.VMEM((size, length, LANES), bf16))
    vmem = pl.BlockSpec(memory_space=pltpu.VMEM)
    hbm = pl.BlockSpec(memory_space=pltpu.HBM)
    loss, grad_att, res = pl.pallas_call(
        functools.partial(kernel, n_grp, n_blk, plan, chunk),
        out_shape=(
            jax.ShapeDtypeStruct((1, queries), f32),
            jax.ShapeDtypeStruct((own_att, dim), f32),
            jax.ShapeDtypeStruct((2, PARTS, rows, LANES), bf16),
        ),
        in_specs=[hbm] * 5,
        out_specs=(vmem,) * 3,
        scratch_shapes=[
            pltpu.VMEM((queries, dim), bf16),
            pltpu.VMEM((dim, dim), bf16),
            pltpu.VMEM((own_att, dim), bf16),
            pltpu.VMEM((1, n_att), jnp.int32),
            pltpu.VMEM((1, queries), jnp.int32),
            pltpu.SemaphoreType.DMA((4 + queries // chunk,)),
            pltpu.VMEM((dim, dim), bf16),
            pltpu.VMEM((dim, queries), bf16),
            pltpu.VMEM((dim, queries), bf16),
            pltpu.VMEM((n_att, queries), bf16),
            pltpu.VMEM((n_att, queries), bf16),
            pltpu.VMEM((1, queries), f32),
            pltpu.VMEM((1, queries), f32),
            pltpu.VMEM((n_att, dim), bf16),
            pltpu.VMEM((dim, n_att), bf16),
            pltpu.VMEM((2, n_blk // 2, own_att, dim), bf16),
            pltpu.VMEM((n_blk // 2, own_att, dim), bf16),
            pltpu.VMEM((n_blk // 2, own_att, dim), bf16),
            pltpu.VMEM((max(n_blk // 2 - 1, 1), own_att, dim), bf16),
            pltpu.VMEM((PARTS, rows, LANES), f32),
            pltpu.VMEM((PARTS, rows, LANES), bf16),
            pltpu.VMEM((PARTS, rows, LANES), bf16),
            pltpu.SemaphoreType.DMA((copies,)),
            pltpu.SemaphoreType.DMA((copies,)),
            *stage_bufs,
        ],
        compiler_params=pltpu.CompilerParams(
            collective_id=0, has_side_effects=True, vmem_limit_bytes=48 * 1024 * 1024
        ),
    )(*[pltpu.with_memory_space_constraint(x, pltpu.HBM) for x in (states, query_weight, attempts, attempt_theorem.reshape(1, n_att), positive.reshape(1, queries))])
    loss, grad_att, grad_w = pl.pallas_call(
        write_out,
        out_shape=(
            jax.ShapeDtypeStruct((1, queries), f32),
            jax.ShapeDtypeStruct((own_att, dim), f32),
            jax.ShapeDtypeStruct((dim, dim), f32),
        ),
        in_specs=[vmem] * 3,
        out_specs=(hbm,) * 3,
        scratch_shapes=[pltpu.VMEM((dim, dim), f32), pltpu.SemaphoreType.DMA((2 + dim // LANES,))],
        compiler_params=pltpu.CompilerParams(vmem_limit_bytes=8 * 1024 * 1024),
    )(loss, grad_att, res)
    return loss.reshape(queries), grad_att, grad_w


def solution(mesh):
    n_grp, n_blk = mesh.shape["grp"], mesh.shape["blk"]
    in_specs = (P(("grp", "blk"), None), P(), P(("grp", "blk"), None), P("grp"), P(("grp", "blk")))
    out_specs = (P(("grp", "blk")), P(("grp", "blk"), None), P())
    return jax.shard_map(
        functools.partial(on_device, n_grp, n_blk),
        mesh=mesh, in_specs=in_specs, out_specs=out_specs, check_vma=False,
    )
```
